256 devices in a mesh: cfg: 8 (over x, y_lo), seq: 32 (over z, y_hi, core).
Axes of the slice: x: 4, y: 4 (y_hi: 2, y_lo: 2; y = y_hi * 2 + y_lo), z: 8, core: 2. Of those that a mesh axis runs over, the one named last changes fastest.
Arguments:
- latent: float32 [8, 2048, 64], P('cfg', 'seq'), may hold values from -6 to 6
- query_key_value: bfloat16 [8, 4096, 6144], P('cfg', 'seq'), may hold values from -8 to 8
- text_kv: bfloat16 [8, 128, 4096], P('cfg'), may hold values from -12 to 12
- text_len: int32 [8], P('cfg'), may hold values from 1 to 128, as said below
- hidden: bfloat16 [8, 4096, 2048], P('cfg', 'seq'), may hold values from -20 to 20
- modulation: float32 [8, 3, 2048], P('cfg'), may hold values from -3 to 3
- out_weight: bfloat16 [2048, 2048], replicated, may hold values from -6 to 6
- final_weight: bfloat16 [2048, 64], replicated, may hold values from -0.125 to 0.125
- guide_table: float32 [12, 3, 2048], replicated, may hold values from -3 to 3
- time_index: int32 [4], replicated, may hold values from 0 to 49
- guide_index: int32 [4], replicated, may hold values from 0 to 11
Outputs:
- latent_next: float32 [8, 2048, 64], P('cfg', 'seq')
- guided_velocity: float32 [8, 2048, 64], P('cfg', 'seq')
- final_grad: float32 [2048, 64], P(('cfg', 'seq'))
- table_grad: float32 [12, 3, 2048], P(None, None, ('cfg', 'seq'))
The draws below stay inside these ranges and needn't reach their ends.
Inputs may be any that keep to these rules, and one draw needn't show every extreme that they name: `text_len`: some branch row uses all 128 text tokens.
All inputs are finite; a program needn't handle non-finite values.
Results may differ from the reference program's by a relative error of at most 0.0055.
Values may be sent and summed in bfloat16 or wider, within the bound.
No kernel may reach another device: no remote copies, remote signals or barrier semaphores. Data moves between devices by JAX's collectives and lax.ppermute only.
A program may use at most 64 MiB of HBM per device.

```python
import jax
import jax.numpy as jnp
from jax import lax

TOK_DEV = 128
TXT = 128
HEADS = 16
HD = 128
DW = 2048
LATC = 64
STEPS = 50
GUIDES = 12
CLIPS = 4
TOKENS = 4096
N_CFG = 8
N_SEQ = 32


def draw_query_key_value(key, part):
    key = jax.random.fold_in(key, 11)
    base_key = jax.random.fold_in(key, 0)
    full_shape = (N_CFG, TOKENS, 3 * HEADS * HD)
    drawn = jnp.clip(jax.random.normal(base_key, full_shape, jnp.float32), -5.0, 5.0)
    return drawn.astype(jnp.bfloat16)


def draw_hidden(key, part):
    key = jax.random.fold_in(key, 23)
    row_key, col_key, noise_key = jax.random.split(key, 3)
    row_scale = jnp.exp(jax.random.uniform(row_key, (N_CFG, TOKENS, 1), jnp.float32, -0.69, 0.69))
    col_scale = jnp.exp(jax.random.uniform(col_key, (N_CFG, 1, DW), jnp.float32, -0.69, 0.69))
    noise = jnp.clip(jax.random.normal(noise_key, (N_CFG, TOKENS, DW), jnp.float32), -5.0, 5.0)
    return (noise * row_scale * col_scale).astype(jnp.bfloat16)


def draw_text_len(key, part):
    key = jax.random.fold_in(key, 37)
    first_key, second_key = jax.random.split(key)
    lengths = jax.random.randint(first_key, (N_CFG,), 1, TXT + 1)
    chosen = jax.random.randint(second_key, (), 0, N_CFG)
    return jnp.where(jnp.arange(N_CFG) == chosen, TXT, lengths).astype(jnp.int32)


def with_ends(entries, own_key, least, top_value):
    dims = entries.shape
    place = [jax.random.randint(jax.random.fold_in(own_key, axis), (), 0, dims[axis]) for axis in range(len(dims))]
    entries = entries.at[tuple(place)].set(least)
    longest = dims.index(max(dims))
    place[longest] = (place[longest] + 1) % dims[longest]
    return entries.at[tuple(place)].set(top_value)


def level_of(own_key, dims, cuts, least, largest):
    loudness = 1.0
    for dim, blocks in cuts:
        draws = jax.random.uniform(jax.random.fold_in(jax.random.fold_in(own_key, 6), dim), (blocks,), jnp.float32, least / len(cuts), largest / len(cuts))
        loudness = loudness * jnp.repeat(jnp.exp(draws), dims[dim] // blocks).reshape((-1,) + (1,) * (len(dims) - 1 - dim))
    return loudness


def scatter_about(own_key, extent, width, reach, pieces=(), dtype=jnp.bfloat16):
    array = jax.random.normal(own_key, extent, jnp.float32) * width
    if len(pieces) > 0:
        array = level_of(own_key, extent, pieces, -0.22, 0.18) * array
    return jnp.clip(array, min=-reach, max=reach).astype(dtype)


def setup_inputs(seed: int = 0) -> dict:
    keys = jax.random.split(jax.random.key(seed), 12)
    return {
        "latent": scatter_about(keys[0], (N_CFG, TOKENS // 2, LATC), 1.0, 6.0, ((0, 8), (1, 32)), jnp.float32),
        "query_key_value": draw_query_key_value(jax.random.fold_in(keys[11], 71), 0),
        "text_kv": scatter_about(keys[2], (N_CFG, TXT, 2 * HEADS * HD), 2.0, 12.0, ((0, 8),)),
        "text_len": draw_text_len(jax.random.fold_in(keys[11], 71), 0),
        "hidden": draw_hidden(jax.random.fold_in(keys[11], 71), 0),
        "modulation": scatter_about(keys[5], (N_CFG, 3, DW), 0.6, 3.0, ((0, 8),), jnp.float32),
        "out_weight": scatter_about(keys[6], (HEADS * HD, DW), ((TOKENS // 2) ** 0.5 * (HEADS * HD) ** -0.5), 6.0),
        "final_weight": scatter_about(keys[7], (DW, LATC), DW ** -0.5, 0.125),
        "guide_table": scatter_about(keys[8], (GUIDES, 3, DW), 0.5, 3.0, (), jnp.float32),
        "time_index": with_ends(jax.random.randint(keys[9], (CLIPS,), 0, STEPS), jax.random.fold_in(keys[9], 1), 0, STEPS - 1).astype(jnp.int32),
        "guide_index": with_ends(jax.random.randint(keys[10], (CLIPS,), 0, GUIDES), jax.random.fold_in(keys[10], 1), 0, GUIDES - 1).astype(jnp.int32),
    }


NORM_EPS = 1e-06
SHIFT_FACTOR = 7.0
GUIDE_STEP = 0.5

def rounded(values):
    return lax.optimization_barrier(values.astype(jnp.bfloat16)).astype(jnp.float32)

def normalize(stream):
    average = lax.optimization_barrier(jnp.mean(stream, axis=-1, keepdims=True))
    centered = stream - average
    inverse = lax.rsqrt(lax.optimization_barrier(jnp.mean(centered * centered, axis=-1, keepdims=True)) + NORM_EPS)
    return (centered * inverse, inverse)

def sigma_at(position):
    frac_left = 1.0 - position / STEPS
    return SHIFT_FACTOR * frac_left / (1.0 + (SHIFT_FACTOR - 1.0) * frac_left)

def head_attention(query, keys_all, values_all, valid):
    count = query.shape[0]
    block = 512 if count % 512 == 0 else count

    def one_block(query_block):
        scores = jnp.dot(query_block, keys_all.T, precision=lax.Precision.HIGHEST) * HD ** (-0.5)
        scores = jnp.where(valid[None, :], scores, -jnp.inf)
        highest = lax.optimization_barrier(jnp.max(scores, axis=1, keepdims=True))
        weights = jnp.exp(scores - highest)
        total = lax.optimization_barrier(jnp.sum(weights, axis=1, keepdims=True))
        mixed = jnp.dot(rounded(weights), values_all, precision=lax.Precision.HIGHEST)
        return (mixed / total).astype(jnp.bfloat16)
    return lax.map(one_block, query.reshape(count // block, block, HD)).reshape(count, HD)

def split_heads(block_rows):
    return block_rows.astype(jnp.float32).reshape(block_rows.shape[0], HEADS, HD).transpose(1, 0, 2)

def branch_attention(packed, text_rows, length):
    head_width = HEADS * HD
    queries = split_heads(packed[:, :head_width])
    keys_all = jnp.concatenate([split_heads(packed[:, head_width:2 * head_width]), split_heads(text_rows[:, :head_width])], axis=1)
    values_all = jnp.concatenate([split_heads(packed[:, 2 * head_width:]), split_heads(text_rows[:, head_width:])], axis=1)
    valid = jnp.arange(TOKENS + TXT) < TOKENS + length

    def one_head(operands):
        return head_attention(operands[0], operands[1], operands[2], valid)
    heads_out = lax.map(one_head, (queries, keys_all, values_all))
    return heads_out.transpose(1, 0, 2).reshape(TOKENS, head_width)

def to_clip_order(pair_rows):
    return pair_rows.reshape(2, N_SEQ, TOK_DEV // 2, LATC).transpose(1, 0, 2, 3).reshape(TOKENS, LATC)

def to_pair_rows(clip_rows):
    return clip_rows.reshape(N_SEQ, 2, TOK_DEV // 2, LATC).transpose(1, 0, 2, 3).reshape(2, TOKENS // 2, LATC)

def reference(latent, query_key_value, text_kv, text_len, hidden, modulation, out_weight, final_weight, guide_table, time_index, guide_index):
    count_scale = 1.0 / (CLIPS * TOKENS)
    out_full = out_weight.astype(jnp.float32)
    final_full = final_weight.astype(jnp.float32)
    next_rows = []
    guided_rows = []
    final_grad = jnp.zeros((DW, LATC), jnp.float32)
    table_grad = jnp.zeros((GUIDES, 3, DW), jnp.float32)
    for clip_index in range(CLIPS):
        velocities = []
        projections = []
        for branch in range(2):
            row_index = 2 * clip_index + branch
            attention = branch_attention(query_key_value[row_index], text_kv[row_index], text_len[row_index])
            projected = rounded(jnp.dot(attention.astype(jnp.float32), out_full, precision=lax.Precision.HIGHEST))
            modul = modulation[row_index]
            stream = hidden[row_index].astype(jnp.float32) + modul[0] * projected
            normed, unused_inverse = normalize(stream)
            shaped = rounded(normed * (1.0 + modul[2]) + modul[1])
            velocities.append(jnp.dot(shaped, final_full, precision=lax.Precision.HIGHEST))
            projections.append(projected)
        cond_vel, uncond_vel = velocities
        factor = 1.0 + GUIDE_STEP * guide_index[clip_index].astype(jnp.float32)
        guided = uncond_vel + factor * (cond_vel - uncond_vel)
        position = time_index[clip_index].astype(jnp.float32)
        step_size = sigma_at(position + 1.0) - sigma_at(position)
        current = to_clip_order(latent[2 * clip_index:2 * clip_index + 2])
        next_rows.append(to_pair_rows(current + step_size * guided))
        guided_rows.append(to_pair_rows(guided))
        student_mod = modulation[2 * clip_index] + guide_table[guide_index[clip_index]]
        student_stream = hidden[2 * clip_index].astype(jnp.float32) + student_mod[0] * projections[0]
        student_norm, student_inverse = normalize(student_stream)
        student_shaped = rounded(student_norm * (1.0 + student_mod[2]) + student_mod[1])
        student_vel = jnp.dot(student_shaped, final_full, precision=lax.Precision.HIGHEST)
        grad_vel = rounded((student_vel - guided) * count_scale)
        final_grad = final_grad + jnp.dot(student_shaped.T, grad_vel, precision=lax.Precision.HIGHEST)
        grad_shaped = jnp.dot(grad_vel, final_full.T, precision=lax.Precision.HIGHEST)
        grad_shift = lax.optimization_barrier(jnp.sum(grad_shaped, axis=0))
        grad_scale = lax.optimization_barrier(jnp.sum(grad_shaped * student_norm, axis=0))
        grad_norm = grad_shaped * (1.0 + student_mod[2])
        grad_stream = student_inverse * (grad_norm - lax.optimization_barrier(jnp.mean(grad_norm, axis=1, keepdims=True)) - student_norm * lax.optimization_barrier(jnp.mean(grad_norm * student_norm, axis=1, keepdims=True)))
        grad_gate = lax.optimization_barrier(jnp.sum(grad_stream * projections[0], axis=0))
        grad_mod = jnp.stack([grad_gate, grad_shift, grad_scale])
        picked = (jnp.arange(GUIDES) == guide_index[clip_index]).astype(jnp.float32)
        table_grad = table_grad + picked[:, None, None] * grad_mod[None]
    latent_next = jnp.concatenate(next_rows, axis=0)
    guided_velocity = jnp.concatenate(guided_rows, axis=0)
    return (latent_next, guided_velocity, final_grad, table_grad)
```

```python
import functools
import math

import jax
import jax.numpy as jnp
from jax import lax
from jax.experimental import pallas as pl
from jax.experimental.pallas import tpu as pltpu
from jax.sharding import PartitionSpec as P

HEADS = 16
HD = 128
STEPS = 50
LATC = 64
NORM_EPS = 1e-06
SHIFT_FACTOR = 7.0
GUIDE_STEP = 0.5

F32 = jnp.float32
BF16 = jnp.bfloat16
VMEM = pl.BlockSpec(memory_space=pltpu.VMEM)
SMEM = pl.BlockSpec(memory_space=pltpu.SMEM)
ANY = pl.BlockSpec(memory_space=pl.ANY)
SCORE_SCALE = HD**-0.5 * math.log2(math.e)
NT = (((1,), (1,)), ((), ()))
TN = (((0,), (0,)), ((), ()))


def sigma_at(position):
    frac_left = 1.0 - position / STEPS
    return SHIFT_FACTOR * frac_left / (1.0 + (SHIFT_FACTOR - 1.0) * frac_left)


def normalize(stream):
    average = jnp.mean(stream, axis=-1, keepdims=True)
    centered = stream - average
    inverse = lax.rsqrt(jnp.mean(centered * centered, axis=-1, keepdims=True) + NORM_EPS)
    return centered * inverse, inverse


QBLOCK = 512


def attend_kernel(own, other, text_k, text_v, length, out, keys, values, scores):
    sources, unused, rows, unused2 = own.shape
    half = sources * rows
    video = 2 * half
    text = text_k.shape[0]
    for index, ref in enumerate((own, other)):
        block = ref[:, 1].reshape(half, HD)
        span = pl.ds(index * half, half)
        keys[span, :HD] = block
        keys[span, HD:] = block
        values[:HD, span] = ref[:, 2].reshape(half, HD).T
    keys[pl.ds(video, text), :HD] = text_k[...]
    keys[pl.ds(video, text), HD:] = text_k[...]
    values[:HD, pl.ds(video, text)] = text_v[...].T
    values[HD:, :] = jnp.ones((values.shape[0] - HD, video + text), BF16)
    kept = lax.broadcasted_iota(jnp.int32, (text, QBLOCK), 0) < length[0]
    step_sources = QBLOCK // rows
    steps = half // QBLOCK

    def score(step, slot):
        first = jnp.minimum(step, steps - 1) * step_sources
        query = own[pl.ds(first, step_sources), 0].reshape(QBLOCK, HD).astype(F32) * SCORE_SCALE
        high = query.astype(BF16)
        low = (query - high.astype(F32)).astype(BF16)
        split = jnp.concatenate([high, low], axis=1)
        got = lax.dot_general(keys[...], split, NT, preferred_element_type=F32)
        scores[slot, :video] = got[:video]
        scores[slot, video:] = jnp.where(kept, got[video:], -jnp.inf)

    def finish(step, slot):
        block = scores[slot]
        highest = jnp.max(block, axis=0, keepdims=True)
        weights = jnp.exp2(block - highest).astype(BF16)
        mixed = jnp.dot(values[...], weights, preferred_element_type=F32)
        result = (mixed[:HD] / mixed[HD : HD + 1]).T.astype(BF16)
        result = result.reshape(step_sources, 2, rows // 2, HD)
        span = pl.ds(step * step_sources, step_sources)
        out[0, span] = result[:, 0]
        out[1, span] = result[:, 1]

    score(0, 0)

    def pair(index, carry):
        score(2 * index + 1, 1)
        finish(2 * index, 0)
        score(2 * index + 2, 0)
        finish(2 * index + 1, 1)
        return carry

    lax.fori_loop(0, steps // 2, pair, 0)


def attend(own, other, text_k, text_v, length):
    sources, unused, rows, unused2 = own.shape
    total = 2 * sources * rows + text_k.shape[0]
    return pl.pallas_call(
        attend_kernel,
        out_shape=jax.ShapeDtypeStruct((2, sources, rows // 2, HD), BF16),
        in_specs=[VMEM, VMEM, VMEM, VMEM, SMEM],
        out_specs=VMEM,
        scratch_shapes=[
            pltpu.VMEM((total, 2 * HD), BF16),
            pltpu.VMEM((HD + 16, total), BF16),
            pltpu.VMEM((2, total, QBLOCK), F32),
        ],
        compiler_params=pltpu.CompilerParams(vmem_limit_bytes=40 << 20),
        cost_estimate=pl.CostEstimate(flops=9 << 30, bytes_accessed=4 << 20, transcendentals=0),
    )(own, other, text_k, text_v, length)


WCHUNKS = 4


def final_kernel(
    flags, factors, heads, weight, own_hid, got_hid, own_mod, got_mod, row, final_t, latent,
    next_out, guided_out, terms_out, attention, held, sems,
    *, count_scale,
):
    width = weight.shape[1]
    chunk = width // WCHUNKS
    copies = [
        pltpu.make_async_copy(weight.at[:, pl.ds(i * chunk, chunk)], held.at[i], sems.at[i])
        for i in range(WCHUNKS)
    ]
    for copy in copies:
        copy.start()
    is_cond = flags[0] == 0
    part = heads.shape[1]
    half = own_hid.shape[0]
    parts = half // part
    for branch in range(2):
        for head in range(HEADS):
            for index in range(parts):
                source = (branch * HEADS + head) * parts + index
                attention[
                    pl.ds(branch * half + index * part, part), pl.ds(head * HD, HD)
                ] = heads[source]
    pieces = []
    for index in range(WCHUNKS):
        copies[index].wait()
        pieces.append(
            jnp.dot(attention[...], held[index], preferred_element_type=F32).astype(BF16)
        )
    projected = jnp.concatenate(pieces, axis=1).astype(F32)
    own_h = own_hid[...].astype(F32)
    got_h = got_hid[...].astype(F32)
    cond_hidden = jnp.where(is_cond, own_h, got_h)
    uncond_hidden = jnp.where(is_cond, got_h, own_h)
    cond_mod = jnp.where(is_cond, own_mod[...], got_mod[...])
    uncond_mod = jnp.where(is_cond, got_mod[...], own_mod[...])
    cond_proj = projected[:half]

    def layer(hidden, proj, mod):
        normed, inverse = normalize(hidden + mod[0:1] * proj)
        shaped = (normed * (1.0 + mod[2:3]) + mod[1:2]).astype(BF16)
        velocity = lax.dot_general(shaped, final_t[...], NT, preferred_element_type=F32)
        return normed, inverse, shaped, velocity

    cond_vel = layer(cond_hidden, cond_proj, cond_mod)[3]
    uncond_vel = layer(uncond_hidden, projected[half:], uncond_mod)[3]
    guided = uncond_vel + factors[0] * (cond_vel - uncond_vel)
    guided_out[...] = guided
    next_out[...] = latent[...] + factors[1] * guided

    mod = cond_mod + row[...]
    normed, inverse, shaped, velocity = layer(cond_hidden, cond_proj, mod)
    grad_vel = ((velocity - guided) * count_scale).astype(BF16)
    grad_shaped = jnp.dot(grad_vel, final_t[...], preferred_element_type=F32)
    grad_shift = jnp.sum(grad_shaped, axis=0, keepdims=True)
    grad_scale = jnp.sum(grad_shaped * normed, axis=0, keepdims=True)
    grad_norm = grad_shaped * (1.0 + mod[2:3])
    grad_stream = inverse * (
        grad_norm
        - jnp.mean(grad_norm, axis=1, keepdims=True)
        - normed * jnp.mean(grad_norm * normed, axis=1, keepdims=True)
    )
    grad_gate = jnp.sum(grad_stream * cond_proj, axis=0, keepdims=True)
    table = jnp.concatenate(
        [grad_gate, grad_shift, grad_scale, jnp.zeros((13, width), F32)], axis=0
    ).astype(BF16)
    left = jnp.concatenate([shaped, table], axis=0)
    lanes = lax.broadcasted_iota(jnp.int32, (16, 2 * LATC), 1)
    lines = lax.broadcasted_iota(jnp.int32, (16, 2 * LATC), 0)
    unit = (lanes == lines + LATC).astype(F32).astype(BF16)
    right = jnp.concatenate(
        [jnp.concatenate([grad_vel, jnp.zeros_like(grad_vel)], axis=1), unit], axis=0
    )
    terms_out[...] = lax.dot_general(left, right, TN, preferred_element_type=F32).astype(BF16)


def final_layer(
    flags, factors, heads, weight, own_hid, got_hid, own_mod, got_mod, row, final_t, latent, count_scale
):
    half, width = own_hid.shape
    return pl.pallas_call(
        functools.partial(final_kernel, count_scale=count_scale),
        out_shape=(
            jax.ShapeDtypeStruct(latent.shape, F32),
            jax.ShapeDtypeStruct(latent.shape, F32),
            jax.ShapeDtypeStruct((width, 2 * LATC), BF16),
        ),
        in_specs=[SMEM, SMEM, VMEM, ANY] + [VMEM] * 7,
        out_specs=(VMEM, VMEM, VMEM),
        scratch_shapes=[
            pltpu.VMEM((2 * half, HEADS * HD), BF16),
            pltpu.VMEM((WCHUNKS, HEADS * HD, width // WCHUNKS), BF16),
            pltpu.SemaphoreType.DMA((WCHUNKS,)),
        ],
        compiler_params=pltpu.CompilerParams(vmem_limit_bytes=32 << 20),
        cost_estimate=pl.CostEstimate(flops=1 << 30, bytes_accessed=10 << 20, transcendentals=0),
    )(flags, factors, heads, weight, own_hid, got_hid, own_mod, got_mod, row, final_t, latent)


def sum_kernel(levels, got, final_out, table_out):
    clips = got.shape[0]
    guides = table_out.shape[2]
    total = None
    planes = [jnp.zeros((8, guides), F32) for unused in range(3)]
    for clip in range(clips):
        block = got[clip].astype(F32).reshape(got.shape[1] // 8, 8, 2 * LATC)
        block = jnp.sum(block, axis=0)
        total = block if total is None else total + block
        picked = lax.broadcasted_iota(jnp.int32, (8, guides), 1) == levels[clip]
        for plane in range(3):
            column = block[:, LATC + plane : LATC + plane + 1]
            planes[plane] = planes[plane] + jnp.where(picked, column, 0.0)
    final_out[...] = total[:, :LATC]
    for plane in range(3):
        table_out[plane] = planes[plane]


def sum_terms(levels, got, guides):
    return pl.pallas_call(
        sum_kernel,
        out_shape=(
            jax.ShapeDtypeStruct((8, LATC), F32),
            jax.ShapeDtypeStruct((3, 8, guides), F32),
        ),
        in_specs=[SMEM, VMEM],
        out_specs=(VMEM, VMEM),
        compiler_params=pltpu.CompilerParams(vmem_limit_bytes=16 << 20),
    )(levels, got)


def local(
    latent,
    query_key_value,
    text_kv,
    text_len,
    hidden,
    modulation,
    out_weight,
    final_weight,
    guide_table,
    time_index,
    guide_index,
):
    seq_count = lax.axis_size("seq")
    cfg_count = lax.axis_size("cfg")
    seq_index = lax.axis_index("seq")
    cfg_index = lax.axis_index("cfg")
    branch = cfg_index % 2
    clip_index = cfg_index // 2
    clips = cfg_count // 2
    tok_rows = query_key_value.shape[1]
    half_rows = tok_rows // 2
    head_width = HEADS * HD
    cores = seq_count // HEADS
    part = half_rows // cores

    sent = query_key_value.reshape(2, cores, part, 3, HEADS, HD).transpose(4, 1, 3, 0, 2, 5)
    sent = sent.reshape(seq_count, 3 * 2 * part, HD)
    got = lax.all_to_all(sent, "seq", split_axis=0, concat_axis=0, tiled=True)
    own = got.reshape(seq_count, 3, 2 * part, HD)
    other = lax.ppermute(own, "seq", [(i, i ^ 1) for i in range(seq_count)])

    pairs = [(i, i ^ 1) for i in range(cfg_count)]
    own_hid = lax.dynamic_slice_in_dim(hidden[0], branch * half_rows, half_rows, 0)
    far_hid = lax.dynamic_slice_in_dim(hidden[0], (1 - branch) * half_rows, half_rows, 0)
    got_hid = lax.ppermute(far_hid, "cfg", pairs)
    own_mod = modulation[0]
    got_mod = lax.ppermute(own_mod, "cfg", pairs)

    head = seq_index // cores
    text_k = lax.dynamic_slice_in_dim(text_kv[0], head * HD, HD, 1)
    text_v = lax.dynamic_slice_in_dim(text_kv[0], head_width + head * HD, HD, 1)
    mixed = attend(own, other, text_k, text_v, text_len)

    members = 2 * seq_count
    groups = [list(range(g * members, (g + 1) * members)) for g in range(clips)]
    heads = lax.all_to_all(
        mixed.reshape(members, part, HD),
        ("cfg", "seq"),
        split_axis=0,
        concat_axis=0,
        tiled=True,
        axis_index_groups=groups,
    )

    level = guide_index[clip_index]
    factor = 1.0 + GUIDE_STEP * level.astype(F32)
    position = time_index[clip_index].astype(F32)
    step_size = sigma_at(position + 1.0) - sigma_at(position)
    row = lax.dynamic_index_in_dim(guide_table, level, 0, keepdims=False)
    count_scale = 1.0 / (clips * tok_rows * seq_count)
    latent_next, guided, terms = final_layer(
        branch.astype(jnp.int32).reshape(1),
        jnp.stack([factor, step_size]),
        heads,
        out_weight,
        own_hid,
        got_hid,
        own_mod,
        got_mod,
        row,
        final_weight.T,
        latent[0],
        count_scale,
    )
    devices = cfg_count * seq_count
    pieces = lax.all_to_all(
        terms.reshape(devices, terms.shape[0] // devices, 2 * LATC),
        ("cfg", "seq"),
        split_axis=0,
        concat_axis=0,
        tiled=True,
    )
    final_grad, table = sum_terms(
        guide_index, pieces.reshape(clips, terms.shape[0] // clips, 2 * LATC), guide_table.shape[0]
    )
    return (latent_next[None], guided[None], final_grad, table.transpose(2, 0, 1))


def solution(mesh):
    in_specs = (
        P("cfg", "seq", None),
        P("cfg", "seq", None),
        P("cfg", None, None),
        P("cfg"),
        P("cfg", "seq", None),
        P("cfg", None, None),
        P(),
        P(),
        P(),
        P(),
        P(),
    )
    out_specs = (
        P("cfg", "seq", None),
        P("cfg", "seq", None),
        P(("cfg", "seq"), None),
        P(None, None, ("cfg", "seq")),
    )
    return jax.shard_map(local, mesh=mesh, in_specs=in_specs, out_specs=out_specs, check_vma=False)
```

```python
import functools
import math

import jax
import jax.numpy as jnp
from jax import lax
from jax.experimental import pallas as pl
from jax.experimental.pallas import tpu as pltpu
from jax.sharding import PartitionSpec as P

HEADS = 16
HD = 128
STEPS = 50
LATC = 64
NORM_EPS = 1e-06
SHIFT_FACTOR = 7.0
GUIDE_STEP = 0.5

F32 = jnp.float32
BF16 = jnp.bfloat16
VMEM = pl.BlockSpec(memory_space=pltpu.VMEM)
SMEM = pl.BlockSpec(memory_space=pltpu.SMEM)
ANY = pl.BlockSpec(memory_space=pl.ANY)
SCORE_SCALE = HD**-0.5 * math.log2(math.e)
NT = (((1,), (1,)), ((), ()))
TN = (((0,), (0,)), ((), ()))


def sigma_at(position):
    frac_left = 1.0 - position / STEPS
    return SHIFT_FACTOR * frac_left / (1.0 + (SHIFT_FACTOR - 1.0) * frac_left)


def normalize(stream):
    average = jnp.mean(stream, axis=-1, keepdims=True)
    centered = stream - average
    inverse = lax.rsqrt(jnp.mean(centered * centered, axis=-1, keepdims=True) + NORM_EPS)
    return centered * inverse, inverse


QBLOCK = 512


def attend_kernel(own, other, text_k, text_v, length, weight, out, staged, keys, values, scores, sem):
    staging = pltpu.make_async_copy(weight, staged, sem)
    staging.start()
    sources, unused, rows, unused2 = own.shape
    half = sources * rows
    video = 2 * half
    text = text_k.shape[0]
    for index, ref in enumerate((own, other)):
        block = ref[:, 1].reshape(half, HD)
        span = pl.ds(index * half, half)
        keys[span, :HD] = block
        keys[span, HD:] = block
        values[:HD, span] = ref[:, 2].reshape(half, HD).T
    keys[pl.ds(video, text), :HD] = text_k[...]
    keys[pl.ds(video, text), HD:] = text_k[...]
    values[:HD, pl.ds(video, text)] = text_v[...].T
    values[HD:, :] = jnp.ones((values.shape[0] - HD, video + text), BF16)
    kept = lax.broadcasted_iota(jnp.int32, (text, QBLOCK), 0) < length[0]
    step_sources = QBLOCK // rows
    steps = half // QBLOCK

    def score(step, slot):
        first = jnp.minimum(step, steps - 1) * step_sources
        query = own[pl.ds(first, step_sources), 0].reshape(QBLOCK, HD).astype(F32) * SCORE_SCALE
        high = query.astype(BF16)
        low = (query - high.astype(F32)).astype(BF16)
        split = jnp.concatenate([high, low], axis=1)
        got = lax.dot_general(keys[...], split, NT, preferred_element_type=F32)
        scores[slot, :video] = got[:video]
        scores[slot, video:] = jnp.where(kept, got[video:], -jnp.inf)

    def finish(step, slot):
        block = scores[slot]
        highest = jnp.max(block, axis=0, keepdims=True)
        weights = jnp.exp2(block - highest).astype(BF16)
        mixed = jnp.dot(values[...], weights, preferred_element_type=F32)
        result = (mixed[:HD] / mixed[HD : HD + 1]).T.astype(BF16)
        result = result.reshape(step_sources, 2, rows // 2, HD)
        span = pl.ds(step * step_sources, step_sources)
        out[0, span] = result[:, 0]
        out[1, span] = result[:, 1]

    score(0, 0)

    def pair(index, carry):
        score(2 * index + 1, 1)
        finish(2 * index, 0)
        score(2 * index + 2, 0)
        finish(2 * index + 1, 1)
        return carry

    lax.fori_loop(0, steps // 2, pair, 0)
    staging.wait()


def attend(own, other, text_k, text_v, length, weight):
    sources, unused, rows, unused2 = own.shape
    total = 2 * sources * rows + text_k.shape[0]
    return pl.pallas_call(
        attend_kernel,
        out_shape=(
            jax.ShapeDtypeStruct((2, sources, rows // 2, HD), BF16),
            pltpu.VMEM(weight.shape, BF16),
        ),
        in_specs=[VMEM, VMEM, VMEM, VMEM, SMEM, ANY],
        out_specs=(VMEM, VMEM),
        scratch_shapes=[
            pltpu.VMEM((total, 2 * HD), BF16),
            pltpu.VMEM((HD + 16, total), BF16),
            pltpu.VMEM((2, total, QBLOCK), F32),
            pltpu.SemaphoreType.DMA,
        ],
        compiler_params=pltpu.CompilerParams(vmem_limit_bytes=40 << 20),
        cost_estimate=pl.CostEstimate(flops=9 << 30, bytes_accessed=12 << 20, transcendentals=0),
    )(own, other, text_k, text_v, length, weight)


def final_kernel(
    flags, factors, heads, weight, own_hid, got_hid, own_mod, got_mod, row, final_t, latent,
    next_out, guided_out, kept_out, sent_out, attention,
    *, count_scale,
):
    width = weight.shape[1]
    is_cond = flags[0] == 0
    half = own_hid.shape[0]
    for branch in range(2):
        for head in range(HEADS):
            attention[pl.ds(branch * half, half), pl.ds(head * HD, HD)] = heads[
                branch * HEADS + head
            ]
    projected = jnp.dot(attention[...], weight[...], preferred_element_type=F32)
    projected = projected.astype(BF16).astype(F32)
    own_h = own_hid[...].astype(F32)
    got_h = got_hid[...].astype(F32)
    cond_hidden = jnp.where(is_cond, own_h, got_h)
    uncond_hidden = jnp.where(is_cond, got_h, own_h)
    cond_mod = jnp.where(is_cond, own_mod[...], got_mod[...])
    uncond_mod = jnp.where(is_cond, got_mod[...], own_mod[...])
    cond_proj = projected[:half]

    def layer(hidden, proj, mod):
        normed, inverse = normalize(hidden + mod[0:1] * proj)
        shaped = (normed * (1.0 + mod[2:3]) + mod[1:2]).astype(BF16)
        velocity = lax.dot_general(shaped, final_t[...], NT, preferred_element_type=F32)
        return normed, inverse, shaped, velocity

    cond_vel = layer(cond_hidden, cond_proj, cond_mod)[3]
    uncond_vel = layer(uncond_hidden, projected[half:], uncond_mod)[3]
    guided = uncond_vel + factors[0] * (cond_vel - uncond_vel)
    guided_out[...] = guided
    next_out[...] = latent[...] + factors[1] * guided

    mod = cond_mod + row[...]
    normed, inverse, shaped, velocity = layer(cond_hidden, cond_proj, mod)
    grad_vel = ((velocity - guided) * count_scale).astype(BF16)
    grad_shaped = jnp.dot(grad_vel, final_t[...], preferred_element_type=F32)
    grad_shift = jnp.sum(grad_shaped, axis=0, keepdims=True)
    grad_scale = jnp.sum(grad_shaped * normed, axis=0, keepdims=True)
    grad_norm = grad_shaped * (1.0 + mod[2:3])
    grad_stream = inverse * (
        grad_norm
        - jnp.mean(grad_norm, axis=1, keepdims=True)
        - normed * jnp.mean(grad_norm * normed, axis=1, keepdims=True)
    )
    grad_gate = jnp.sum(grad_stream * cond_proj, axis=0, keepdims=True)
    table = jnp.concatenate(
        [grad_gate, grad_shift, grad_scale, jnp.zeros((13, width), F32)], axis=0
    ).astype(BF16)
    left = jnp.concatenate([shaped, table], axis=0)
    lanes = lax.broadcasted_iota(jnp.int32, (16, 2 * LATC), 1)
    lines = lax.broadcasted_iota(jnp.int32, (16, 2 * LATC), 0)
    unit = (lanes == lines + LATC).astype(F32).astype(BF16)
    right = jnp.concatenate(
        [jnp.concatenate([grad_vel, jnp.zeros_like(grad_vel)], axis=1), unit], axis=0
    )
    terms = lax.dot_general(left, right, TN, preferred_element_type=F32)
    terms = terms.reshape(width // 16, 2, 8, 2 * LATC)
    first = terms[:, 0].reshape(width // 2, 2 * LATC)
    second = terms[:, 1].reshape(width // 2, 2 * LATC)
    on_first = flags[1] == 0
    kept_out[...] = jnp.where(on_first, first, second)
    sent_out[...] = jnp.where(on_first, second, first).astype(BF16)


def final_layer(
    flags, factors, heads, weight, own_hid, got_hid, own_mod, got_mod, row, final_t, latent, count_scale
):
    half, width = own_hid.shape
    return pl.pallas_call(
        functools.partial(final_kernel, count_scale=count_scale),
        out_shape=(
            jax.ShapeDtypeStruct(latent.shape, F32),
            jax.ShapeDtypeStruct(latent.shape, F32),
            jax.ShapeDtypeStruct((width // 2, 2 * LATC), F32),
            jax.ShapeDtypeStruct((width // 2, 2 * LATC), BF16),
        ),
        in_specs=[SMEM, SMEM] + [VMEM] * 9,
        out_specs=(VMEM, VMEM, VMEM, VMEM),
        scratch_shapes=[pltpu.VMEM((2 * half, HEADS * HD), BF16)],
        compiler_params=pltpu.CompilerParams(vmem_limit_bytes=32 << 20),
        cost_estimate=pl.CostEstimate(flops=1 << 30, bytes_accessed=10 << 20, transcendentals=0),
    )(flags, factors, heads, weight, own_hid, got_hid, own_mod, got_mod, row, final_t, latent)


def sum_kernel(levels, got, final_out, table_out):
    clips = got.shape[0]
    guides = table_out.shape[2]
    total = None
    planes = [jnp.zeros((8, guides), F32) for unused in range(3)]
    for clip in range(clips):
        block = got[clip].astype(F32).reshape(got.shape[1] // 8, 8, 2 * LATC)
        block = jnp.sum(block, axis=0)
        total = block if total is None else total + block
        picked = lax.broadcasted_iota(jnp.int32, (8, guides), 1) == levels[clip]
        for plane in range(3):
            column = block[:, LATC + plane : LATC + plane + 1]
            planes[plane] = planes[plane] + jnp.where(picked, column, 0.0)
    final_out[...] = total[:, :LATC]
    for plane in range(3):
        table_out[plane] = planes[plane]


def sum_terms(levels, got, guides):
    return pl.pallas_call(
        sum_kernel,
        out_shape=(
            jax.ShapeDtypeStruct((8, LATC), F32),
            jax.ShapeDtypeStruct((3, 8, guides), F32),
        ),
        in_specs=[SMEM, VMEM],
        out_specs=(VMEM, VMEM),
        compiler_params=pltpu.CompilerParams(vmem_limit_bytes=16 << 20),
    )(levels, got)


def local(
    latent,
    query_key_value,
    text_kv,
    text_len,
    hidden,
    modulation,
    out_weight,
    final_weight,
    guide_table,
    time_index,
    guide_index,
):
    seq_count = lax.axis_size("seq")
    cfg_count = lax.axis_size("cfg")
    seq_index = lax.axis_index("seq")
    cfg_index = lax.axis_index("cfg")
    branch = cfg_index % 2
    clip_index = cfg_index // 2
    clips = cfg_count // 2
    tok_rows = query_key_value.shape[1]
    half_rows = tok_rows // 2
    head_width = HEADS * HD
    cores = seq_count // HEADS

    sent = query_key_value.reshape(tok_rows, 3, HEADS, HD).transpose(2, 1, 0, 3)
    same_core = [[cores * i + core for i in range(HEADS)] for core in range(cores)]
    got = lax.all_to_all(
        sent.reshape(HEADS, 3 * tok_rows, HD),
        "seq",
        split_axis=0,
        concat_axis=0,
        tiled=True,
        axis_index_groups=same_core,
    )
    own = got.reshape(HEADS, 3, tok_rows, HD)
    other = lax.ppermute(own, "seq", [(i, i ^ 1) for i in range(seq_count)])

    pairs = [(i, i ^ 1) for i in range(cfg_count)]
    own_hid = lax.dynamic_slice_in_dim(hidden[0], branch * half_rows, half_rows, 0)
    far_hid = lax.dynamic_slice_in_dim(hidden[0], (1 - branch) * half_rows, half_rows, 0)
    got_hid = lax.ppermute(far_hid, "cfg", pairs)
    own_mod = modulation[0]
    got_mod = lax.ppermute(own_mod, "cfg", pairs)

    head = seq_index // cores
    text_k = lax.dynamic_slice_in_dim(text_kv[0], head * HD, HD, 1)
    text_v = lax.dynamic_slice_in_dim(text_kv[0], head_width + head * HD, HD, 1)
    mixed, weight = attend(own, other, text_k, text_v, text_len, out_weight)

    members = 2 * HEADS
    groups = [
        [(g * members + i) * cores + core for i in range(members)]
        for g in range(clips)
        for core in range(cores)
    ]
    heads = lax.all_to_all(
        mixed.reshape(members, half_rows, HD),
        ("cfg", "seq"),
        split_axis=0,
        concat_axis=0,
        tiled=True,
        axis_index_groups=groups,
    )

    level = guide_index[clip_index]
    factor = 1.0 + GUIDE_STEP * level.astype(F32)
    position = time_index[clip_index].astype(F32)
    step_size = sigma_at(position + 1.0) - sigma_at(position)
    row = lax.dynamic_index_in_dim(guide_table, level, 0, keepdims=False)
    count_scale = 1.0 / (clips * tok_rows * seq_count)
    latent_next, guided, kept, passed = final_layer(
        jnp.stack([branch, seq_index % cores]).astype(jnp.int32),
        jnp.stack([factor, step_size]),
        heads,
        weight,
        own_hid,
        got_hid,
        own_mod,
        got_mod,
        row,
        final_weight.T,
        latent[0],
        count_scale,
    )
    gained = lax.ppermute(passed, "seq", [(i, i ^ 1) for i in range(seq_count)])
    chips = cfg_count * seq_count // cores
    terms = (kept + gained.astype(F32)).astype(BF16)
    pieces = lax.all_to_all(
        terms.reshape(chips, terms.shape[0] // chips, 2 * LATC),
        ("cfg", "seq"),
        split_axis=0,
        concat_axis=0,
        tiled=True,
        axis_index_groups=[[cores * i + core for i in range(chips)] for core in range(cores)],
    )
    final_grad, table = sum_terms(
        guide_index, pieces.reshape(clips, terms.shape[0] // clips, 2 * LATC), guide_table.shape[0]
    )
    return (latent_next[None], guided[None], final_grad, table.transpose(2, 0, 1))


def solution(mesh):
    in_specs = (
        P("cfg", "seq", None),
        P("cfg", "seq", None),
        P("cfg", None, None),
        P("cfg"),
        P("cfg", "seq", None),
        P("cfg", None, None),
        P(),
        P(),
        P(),
        P(),
        P(),
    )
    out_specs = (
        P("cfg", "seq", None),
        P("cfg", "seq", None),
        P(("cfg", "seq"), None),
        P(None, None, ("cfg", "seq")),
    )
    return jax.shard_map(local, mesh=mesh, in_specs=in_specs, out_specs=out_specs, check_vma=False)
```

```python
import functools
import math

import jax
import jax.numpy as jnp
from jax import lax
from jax.experimental import pallas as pl
from jax.experimental.pallas import tpu as pltpu
from jax.sharding import PartitionSpec as P

HEADS = 16
HD = 128
STEPS = 50
LATC = 64
NORM_EPS = 1e-06
SHIFT_FACTOR = 7.0
GUIDE_STEP = 0.5

F32 = jnp.float32
BF16 = jnp.bfloat16
VMEM = pl.BlockSpec(memory_space=pltpu.VMEM)
SMEM = pl.BlockSpec(memory_space=pltpu.SMEM)
ANY = pl.BlockSpec(memory_space=pl.ANY)
HBM = pl.BlockSpec(memory_space=pltpu.HBM)
SCORE_SCALE = HD**-0.5 * math.log2(math.e)
NT = (((1,), (1,)), ((), ()))
TN = (((0,), (0,)), ((), ()))


def sigma_at(position):
    frac_left = 1.0 - position / STEPS
    return SHIFT_FACTOR * frac_left / (1.0 + (SHIFT_FACTOR - 1.0) * frac_left)


def normalize(stream):
    average = jnp.mean(stream, axis=-1, keepdims=True)
    centered = stream - average
    inverse = lax.rsqrt(jnp.mean(centered * centered, axis=-1, keepdims=True) + NORM_EPS)
    return centered * inverse, inverse


def pack_kernel(packed, hidden, modulation, sent, passed, rows_of_mod, sems, late):
    heads, kinds, rows, unused = sent.shape
    half = hidden.shape[1] // 2
    copies = []
    for kind in range(kinds):
        for head in range(heads):
            column = (kind * heads + head) * HD
            copies.append(
                pltpu.make_async_copy(
                    packed.at[0, :, pl.ds(column, HD)],
                    sent.at[head, kind],
                    sems.at[kind * heads + head],
                )
            )
    for copy in copies:
        copy.start()
    far = pl.multiple_of((1 - lax.axis_index("cfg") % 2) * half, half)
    rest = pltpu.make_async_copy(
        hidden.at[0, pl.ds(far, half)], passed.at[pl.ds(0, half)], late.at[0]
    )
    rest.start()
    fetch = pltpu.make_async_copy(modulation, rows_of_mod, late.at[1])
    fetch.start()
    fetch.wait()
    mod = jnp.concatenate([rows_of_mod[0], rows_of_mod[1], rows_of_mod[2]], axis=0)
    high = mod.astype(BF16).astype(F32)
    zeros = jnp.zeros((5, mod.shape[1]), F32)
    parts = jnp.concatenate([high, zeros, mod - high, zeros], axis=0)
    passed[pl.ds(half, 16)] = parts.astype(BF16)
    for copy in copies:
        copy.wait()
    rest.wait()


def pack(packed, hidden, modulation):
    rows = packed.shape[1]
    width = hidden.shape[2]
    packed, hidden, modulation = (
        pltpu.with_memory_space_constraint(array, pltpu.HBM)
        for array in (packed, hidden, modulation)
    )
    return pl.pallas_call(
        pack_kernel,
        out_shape=(
            pltpu.VMEM((HEADS, 3, rows, HD), BF16),
            pltpu.VMEM((rows // 2 + 16, width), BF16),
        ),
        in_specs=[HBM, HBM, HBM],
        out_specs=(VMEM, VMEM),
        scratch_shapes=[
            pltpu.VMEM(modulation.shape, F32),
            pltpu.SemaphoreType.DMA((3 * HEADS,)),
            pltpu.SemaphoreType.DMA((2,)),
        ],
        compiler_params=pltpu.CompilerParams(vmem_limit_bytes=16 << 20),
    )(packed, hidden, modulation)


QBLOCK = 512


def attend_kernel(
    own, other, text_kv, length, weight, out, staged, keys, values, scores, text, sems
):
    head = lax.axis_index("seq") // (lax.axis_size("seq") // HEADS)
    text_copies = [
        pltpu.make_async_copy(
            text_kv.at[0, :, pl.ds(pl.multiple_of((kind * HEADS + head) * HD, HD), HD)],
            text.at[kind],
            sems.at[1 + kind],
        )
        for kind in range(2)
    ]
    for copy in text_copies:
        copy.start()
    staging = pltpu.make_async_copy(weight, staged, sems.at[0])
    staging.start()
    sources, unused, rows, unused2 = own.shape
    half = sources * rows
    video = 2 * half
    words = text.shape[1]
    for index, ref in enumerate((own, other)):
        block = ref[:, 1].reshape(half, HD)
        span = pl.ds(index * half, half)
        keys[span, :HD] = block
        keys[span, HD:] = block
        values[:HD, span] = ref[:, 2].reshape(half, HD).T
    for copy in text_copies:
        copy.wait()
    keys[pl.ds(video, words), :HD] = text[0]
    keys[pl.ds(video, words), HD:] = text[0]
    values[:HD, pl.ds(video, words)] = text[1].T
    values[HD:, :] = jnp.ones((values.shape[0] - HD, video + words), BF16)
    kept = lax.broadcasted_iota(jnp.int32, (words, QBLOCK), 0) < length[0]
    step_sources = QBLOCK // rows
    steps = half // QBLOCK

    def score(step, slot):
        first = jnp.minimum(step, steps - 1) * step_sources
        query = own[pl.ds(first, step_sources), 0].reshape(QBLOCK, HD).astype(F32) * SCORE_SCALE
        high = query.astype(BF16)
        low = (query - high.astype(F32)).astype(BF16)
        split = jnp.concatenate([high, low], axis=1)
        got = lax.dot_general(keys[...], split, NT, preferred_element_type=F32)
        scores[slot, :video] = got[:video]
        scores[slot, video:] = jnp.where(kept, got[video:], -jnp.inf)

    def finish(step, slot):
        block = scores[slot]
        highest = jnp.max(block, axis=0, keepdims=True)
        weights = jnp.exp2(block - highest).astype(BF16)
        mixed = jnp.dot(values[...], weights, preferred_element_type=F32)
        result = (mixed[:HD] / mixed[HD : HD + 1]).T.astype(BF16)
        result = result.reshape(step_sources, 2, rows // 2, HD)
        span = pl.ds(step * step_sources, step_sources)
        out[0, span] = result[:, 0]
        out[1, span] = result[:, 1]

    score(0, 0)

    def pair(index, carry):
        score(2 * index + 1, 1)
        finish(2 * index, 0)
        score(2 * index + 2, 0)
        finish(2 * index + 1, 1)
        return carry

    lax.fori_loop(0, steps // 2, pair, 0)
    staging.wait()


def attend(own, other, text_kv, length, weight):
    sources, unused, rows, unused2 = own.shape
    words = text_kv.shape[1]
    total = 2 * sources * rows + words
    return pl.pallas_call(
        attend_kernel,
        out_shape=(
            jax.ShapeDtypeStruct((2, sources, rows // 2, HD), BF16),
            pltpu.VMEM(weight.shape, BF16),
        ),
        in_specs=[VMEM, VMEM, ANY, SMEM, ANY],
        out_specs=(VMEM, VMEM),
        scratch_shapes=[
            pltpu.VMEM((total, 2 * HD), BF16),
            pltpu.VMEM((HD + 16, total), BF16),
            pltpu.VMEM((2, total, QBLOCK), F32),
            pltpu.VMEM((2, words, HD), BF16),
            pltpu.SemaphoreType.DMA((3,)),
        ],
        compiler_params=pltpu.CompilerParams(vmem_limit_bytes=40 << 20),
        cost_estimate=pl.CostEstimate(flops=9 << 30, bytes_accessed=12 << 20, transcendentals=0),
    )(own, other, text_kv, length, weight)


def final_kernel(
    levels, times, heads, weight, hidden, got, modulation, guide_table, final_t, latent,
    next_out, guided_out, kept_out, sent_out, attention,
    *, count_scale,
):
    width = weight.shape[1]
    cfg_index = lax.axis_index("cfg")
    core = lax.axis_index("seq") % (lax.axis_size("seq") // HEADS)
    branch = cfg_index % 2
    is_cond = branch == 0
    level = levels[cfg_index // 2]
    half = hidden.shape[1] // 2
    for side in range(2):
        for head in range(HEADS):
            attention[pl.ds(side * half, half), pl.ds(head * HD, HD)] = heads[
                side * HEADS + head
            ]
    projected = jnp.dot(attention[...], weight[...], preferred_element_type=F32)
    projected = projected.astype(BF16).astype(F32)
    own_h = hidden[0, pl.ds(pl.multiple_of(branch * half, half), half)].astype(F32)
    got_h = got[:half].astype(F32)
    own_mod = jnp.concatenate([modulation[0], modulation[1], modulation[2]], axis=0)
    parts = got[half:].astype(F32)
    got_mod = parts[:3] + parts[8:11]
    cond_hidden = jnp.where(is_cond, own_h, got_h)
    uncond_hidden = jnp.where(is_cond, got_h, own_h)
    cond_mod = jnp.where(is_cond, own_mod, got_mod)
    uncond_mod = jnp.where(is_cond, got_mod, own_mod)
    cond_proj = projected[:half]

    def layer(hidden, proj, mod):
        normed, inverse = normalize(hidden + mod[0:1] * proj)
        shaped = (normed * (1.0 + mod[2:3]) + mod[1:2]).astype(BF16)
        velocity = lax.dot_general(shaped, final_t[...], NT, preferred_element_type=F32)
        return normed, inverse, shaped, velocity

    cond_vel = layer(cond_hidden, cond_proj, cond_mod)[3]
    uncond_vel = layer(uncond_hidden, projected[half:], uncond_mod)[3]
    factor = 1.0 + GUIDE_STEP * level.astype(F32)
    guided = uncond_vel + factor * (cond_vel - uncond_vel)
    guided_out[0] = guided
    position = jnp.full(guided.shape, times[cfg_index // 2].astype(F32))
    next_out[0] = latent[0] + (sigma_at(position + 1.0) - sigma_at(position)) * guided

    mod = cond_mod + guide_table[level]
    normed, inverse, shaped, velocity = layer(cond_hidden, cond_proj, mod)
    grad_vel = ((velocity - guided) * count_scale).astype(BF16)
    grad_shaped = jnp.dot(grad_vel, final_t[...], preferred_element_type=F32)
    grad_shift = jnp.sum(grad_shaped, axis=0, keepdims=True)
    grad_scale = jnp.sum(grad_shaped * normed, axis=0, keepdims=True)
    grad_norm = grad_shaped * (1.0 + mod[2:3])
    grad_stream = inverse * (
        grad_norm
        - jnp.mean(grad_norm, axis=1, keepdims=True)
        - normed * jnp.mean(grad_norm * normed, axis=1, keepdims=True)
    )
    grad_gate = jnp.sum(grad_stream * cond_proj, axis=0, keepdims=True)
    table = jnp.concatenate(
        [grad_gate, grad_shift, grad_scale, jnp.zeros((13, width), F32)], axis=0
    ).astype(BF16)
    left = jnp.concatenate([shaped, table], axis=0)
    lanes = lax.broadcasted_iota(jnp.int32, (16, 2 * LATC), 1)
    lines = lax.broadcasted_iota(jnp.int32, (16, 2 * LATC), 0)
    unit = (lanes == lines + LATC).astype(F32).astype(BF16)
    right = jnp.concatenate(
        [jnp.concatenate([grad_vel, jnp.zeros_like(grad_vel)], axis=1), unit], axis=0
    )
    terms = lax.dot_general(left, right, TN, preferred_element_type=F32)
    terms = terms.reshape(width // 16, 2, 8, 2 * LATC)
    first = terms[:, 0].reshape(width // 2, 2 * LATC)
    second = terms[:, 1].reshape(width // 2, 2 * LATC)
    on_first = core == 0
    kept_out[...] = jnp.where(on_first, first, second)
    sent_out[...] = jnp.where(on_first, second, first).astype(BF16)


def final_layer(
    levels, times, heads, weight, hidden, got, modulation, guide_table, final_t, latent, count_scale
):
    width = hidden.shape[2]
    half = hidden.shape[1] // 2
    return pl.pallas_call(
        functools.partial(final_kernel, count_scale=count_scale),
        out_shape=(
            jax.ShapeDtypeStruct(latent.shape, F32),
            jax.ShapeDtypeStruct(latent.shape, F32),
            jax.ShapeDtypeStruct((width // 2, 2 * LATC), F32),
            jax.ShapeDtypeStruct((width // 2, 2 * LATC), BF16),
        ),
        in_specs=[SMEM, SMEM] + [VMEM] * 8,
        out_specs=(VMEM, VMEM, VMEM, VMEM),
        scratch_shapes=[pltpu.VMEM((2 * half, HEADS * HD), BF16)],
        compiler_params=pltpu.CompilerParams(vmem_limit_bytes=32 << 20),
        cost_estimate=pl.CostEstimate(flops=1 << 30, bytes_accessed=10 << 20, transcendentals=0),
    )(levels, times, heads, weight, hidden, got, modulation, guide_table, final_t, latent)


def sum_kernel(levels, got, final_out, table_out):
    clips = got.shape[0]
    guides = table_out.shape[2]
    total = None
    planes = [jnp.zeros((8, guides), F32) for unused in range(3)]
    for clip in range(clips):
        block = got[clip].astype(F32).reshape(got.shape[1] // 8, 8, 2 * LATC)
        block = jnp.sum(block, axis=0)
        total = block if total is None else total + block
        picked = lax.broadcasted_iota(jnp.int32, (8, guides), 1) == levels[clip]
        for plane in range(3):
            column = block[:, LATC + plane : LATC + plane + 1]
            planes[plane] = planes[plane] + jnp.where(picked, column, 0.0)
    final_out[...] = total[:, :LATC]
    for plane in range(3):
        table_out[plane] = planes[plane]


def sum_terms(levels, got, guides):
    return pl.pallas_call(
        sum_kernel,
        out_shape=(
            jax.ShapeDtypeStruct((8, LATC), F32),
            jax.ShapeDtypeStruct((3, 8, guides), F32),
        ),
        in_specs=[SMEM, VMEM],
        out_specs=(VMEM, VMEM),
        compiler_params=pltpu.CompilerParams(vmem_limit_bytes=16 << 20),
    )(levels, got)


def local(
    latent,
    query_key_value,
    text_kv,
    text_len,
    hidden,
    modulation,
    out_weight,
    final_weight,
    guide_table,
    time_index,
    guide_index,
):
    seq_count = lax.axis_size("seq")
    cfg_count = lax.axis_size("cfg")
    clips = cfg_count // 2
    tok_rows = query_key_value.shape[1]
    half_rows = tok_rows // 2
    cores = seq_count // HEADS
    mod_rows = modulation.transpose(1, 0, 2)

    sent, passed = pack(query_key_value, hidden, mod_rows)
    same_core = [[cores * i + core for i in range(HEADS)] for core in range(cores)]
    got = lax.all_to_all(
        sent.reshape(HEADS, 3 * tok_rows, HD),
        "seq",
        split_axis=0,
        concat_axis=0,
        tiled=True,
        axis_index_groups=same_core,
    )
    own = got.reshape(HEADS, 3, tok_rows, HD)
    other = lax.ppermute(own, "seq", [(i, i ^ 1) for i in range(seq_count)])
    gotten = lax.ppermute(passed, "cfg", [(i, i ^ 1) for i in range(cfg_count)])
    mixed, weight = attend(own, other, text_kv, text_len, out_weight)
    mixed, gotten = lax.optimization_barrier((mixed, gotten))

    members = 2 * HEADS
    groups = [
        [(g * members + i) * cores + core for i in range(members)]
        for g in range(clips)
        for core in range(cores)
    ]
    heads = lax.all_to_all(
        mixed.reshape(members, half_rows, HD),
        ("cfg", "seq"),
        split_axis=0,
        concat_axis=0,
        tiled=True,
        axis_index_groups=groups,
    )

    count_scale = 1.0 / (clips * tok_rows * seq_count)
    latent_next, guided, kept, given = final_layer(
        guide_index,
        time_index,
        heads,
        weight,
        hidden,
        gotten,
        mod_rows,
        guide_table,
        final_weight.T,
        latent,
        count_scale,
    )
    gained = lax.ppermute(given, "seq", [(i, i ^ 1) for i in range(seq_count)])
    chips = cfg_count * seq_count // cores
    terms = (kept + gained.astype(F32)).astype(BF16)
    pieces = lax.all_to_all(
        terms.reshape(chips, terms.shape[0] // chips, 2 * LATC),
        ("cfg", "seq"),
        split_axis=0,
        concat_axis=0,
        tiled=True,
        axis_index_groups=[[cores * i + core for i in range(chips)] for core in range(cores)],
    )
    final_grad, table = sum_terms(
        guide_index, pieces.reshape(clips, terms.shape[0] // clips, 2 * LATC), guide_table.shape[0]
    )
    return (latent_next, guided, final_grad, table.transpose(2, 0, 1))


def solution(mesh):
    in_specs = (
        P("cfg", "seq", None),
        P("cfg", "seq", None),
        P("cfg", None, None),
        P("cfg"),
        P("cfg", "seq", None),
        P("cfg", None, None),
        P(),
        P(),
        P(),
        P(),
        P(),
    )
    out_specs = (
        P("cfg", "seq", None),
        P("cfg", "seq", None),
        P(("cfg", "seq"), None),
        P(None, None, ("cfg", "seq")),
    )
    return jax.shard_map(local, mesh=mesh, in_specs=in_specs, out_specs=out_specs, check_vma=False)
```

```python
import functools
import math

import jax
import jax.numpy as jnp
from jax import lax
from jax.experimental import pallas as pl
from jax.experimental.pallas import tpu as pltpu
from jax.sharding import PartitionSpec as P

HEADS = 16
HD = 128
STEPS = 50
LATC = 64
NORM_EPS = 1e-06
SHIFT_FACTOR = 7.0
GUIDE_STEP = 0.5

F32 = jnp.float32
BF16 = jnp.bfloat16
VMEM = pl.BlockSpec(memory_space=pltpu.VMEM)
SMEM = pl.BlockSpec(memory_space=pltpu.SMEM)
ANY = pl.BlockSpec(memory_space=pl.ANY)
HBM = pl.BlockSpec(memory_space=pltpu.HBM)
SCORE_SCALE = HD**-0.5 * math.log2(math.e)
NT = (((1,), (1,)), ((), ()))
TN = (((0,), (0,)), ((), ()))


def sigma_at(position):
    frac_left = 1.0 - position / STEPS
    return SHIFT_FACTOR * frac_left / (1.0 + (SHIFT_FACTOR - 1.0) * frac_left)


def normalize(stream):
    average = jnp.mean(stream, axis=-1, keepdims=True)
    centered = stream - average
    inverse = lax.rsqrt(jnp.mean(centered * centered, axis=-1, keepdims=True) + NORM_EPS)
    return centered * inverse, inverse


def pack_kernel(packed, hidden, modulation, sent, passed, rows_of_mod, sems, late):
    heads, kinds, rows, unused = sent.shape
    half = hidden.shape[1] // 2
    copies = []
    for kind in range(kinds):
        for head in range(heads):
            column = (kind * heads + head) * HD
            copies.append(
                pltpu.make_async_copy(
                    packed.at[0, :, pl.ds(column, HD)],
                    sent.at[head, kind],
                    sems.at[kind * heads + head],
                )
            )
    for copy in copies:
        copy.start()
    far = pl.multiple_of((1 - lax.axis_index("cfg") % 2) * half, half)
    rest = pltpu.make_async_copy(
        hidden.at[0, pl.ds(far, half)], passed.at[pl.ds(0, half)], late.at[0]
    )
    rest.start()
    fetch = pltpu.make_async_copy(modulation, rows_of_mod, late.at[1])
    fetch.start()
    fetch.wait()
    mod = jnp.concatenate([rows_of_mod[0], rows_of_mod[1], rows_of_mod[2]], axis=0)
    high = mod.astype(BF16).astype(F32)
    zeros = jnp.zeros((5, mod.shape[1]), F32)
    parts = jnp.concatenate([high, zeros, mod - high, zeros], axis=0)
    passed[pl.ds(half, 16)] = parts.astype(BF16)
    for copy in copies:
        copy.wait()
    rest.wait()


def pack(packed, hidden, modulation):
    rows = packed.shape[1]
    width = hidden.shape[2]
    packed, hidden, modulation = (
        pltpu.with_memory_space_constraint(array, pltpu.HBM)
        for array in (packed, hidden, modulation)
    )
    return pl.pallas_call(
        pack_kernel,
        out_shape=(
            pltpu.VMEM((HEADS, 3, rows, HD), BF16),
            pltpu.VMEM((rows // 2 + 16, width), BF16),
        ),
        in_specs=[HBM, HBM, HBM],
        out_specs=(VMEM, VMEM),
        scratch_shapes=[
            pltpu.VMEM(modulation.shape, F32),
            pltpu.SemaphoreType.DMA((3 * HEADS,)),
            pltpu.SemaphoreType.DMA((2,)),
        ],
        compiler_params=pltpu.CompilerParams(vmem_limit_bytes=16 << 20),
    )(packed, hidden, modulation)


QBLOCK = 512


def split_query(own, first, count):
    query = own[pl.ds(first, count), 0].reshape(QBLOCK, HD).astype(F32) * SCORE_SCALE
    high = query.astype(BF16)
    low = (query - high.astype(F32)).astype(BF16)
    return jnp.concatenate([high, low], axis=1)


def place_pair(keys, values, first, key, value):
    span = pl.ds(first, key.shape[0])
    keys[span, :HD] = key
    keys[span, HD:] = key
    values[:HD, span] = value.T


def run_steps(steps, score, finish):
    score(0, 0)
    for step in range(steps):
        if step + 1 < steps:
            score(step + 1, (step + 1) % 2)
        finish(step, step % 2)


def near_kernel(own, state, keys, values, scores, tops):
    sources, unused, rows, unused2 = own.shape
    video = sources * rows
    place_pair(keys, values, 0, own[:, 1].reshape(video, HD), own[:, 2].reshape(video, HD))
    values[HD:, :] = jnp.ones((values.shape[0] - HD, video), BF16)
    count = QBLOCK // rows

    def score(step, slot):
        got = lax.dot_general(
            keys[...], split_query(own, step * count, count), NT, preferred_element_type=F32
        )
        scores[slot] = got
        tops[slot] = jnp.max(got, axis=0, keepdims=True)

    def finish(step, slot):
        highest = tops[slot]
        weights = jnp.exp2(scores[slot] - highest).astype(BF16)
        mixed = jnp.dot(values[...], weights, preferred_element_type=F32)
        span = pl.ds(step * QBLOCK, QBLOCK)
        state[: HD + 8, span] = mixed[: HD + 8]
        state[HD + 8 :, span] = jnp.broadcast_to(highest, (8, QBLOCK))

    run_steps(video // QBLOCK, score, finish)


def far_kernel(
    own, other, state, text_kv, length, weight, out, staged, keys, values, scores, tops, text, sems
):
    head = lax.axis_index("seq") // (lax.axis_size("seq") // HEADS)
    text_copies = [
        pltpu.make_async_copy(
            text_kv.at[0, :, pl.ds(pl.multiple_of((kind * HEADS + head) * HD, HD), HD)],
            text.at[kind],
            sems.at[1 + kind],
        )
        for kind in range(2)
    ]
    for copy in text_copies:
        copy.start()
    staging = pltpu.make_async_copy(weight, staged, sems.at[0])
    staging.start()
    sources, unused, rows, unused2 = own.shape
    video = sources * rows
    words = text.shape[1]
    place_pair(keys, values, 0, other[:, 1].reshape(video, HD), other[:, 2].reshape(video, HD))
    for copy in text_copies:
        copy.wait()
    place_pair(keys, values, video, text[0], text[1])
    values[HD:, :] = jnp.ones((values.shape[0] - HD, video + words), BF16)
    kept = lax.broadcasted_iota(jnp.int32, (words, QBLOCK), 0) < length[0]
    count = QBLOCK // rows

    def score(step, slot):
        got = lax.dot_general(
            keys[...], split_query(own, step * count, count), NT, preferred_element_type=F32
        )
        masked = jnp.where(kept, got[video:], -jnp.inf)
        scores[slot, :video] = got[:video]
        scores[slot, video:] = masked
        tops[slot] = jnp.maximum(
            jnp.max(got[:video], axis=0, keepdims=True), jnp.max(masked, axis=0, keepdims=True)
        )

    def finish(step, slot):
        span = pl.ds(step * QBLOCK, QBLOCK)
        before = state[HD + 8 : HD + 9, span]
        highest = jnp.maximum(tops[slot], before)
        weights = jnp.exp2(scores[slot] - highest).astype(BF16)
        mixed = jnp.dot(values[...], weights, preferred_element_type=F32)
        mixed = mixed[: HD + 8] + state[: HD + 8, span] * jnp.exp2(before - highest)
        result = (mixed[:HD] / mixed[HD : HD + 1]).T.astype(BF16)
        result = result.reshape(count, 2, rows // 2, HD)
        span = pl.ds(step * count, count)
        out[0, span] = result[:, 0]
        out[1, span] = result[:, 1]

    run_steps(video // QBLOCK, score, finish)
    staging.wait()


def attend_near(own):
    sources, unused, rows, unused2 = own.shape
    total = sources * rows
    return pl.pallas_call(
        near_kernel,
        out_shape=jax.ShapeDtypeStruct((HD + 16, total), F32),
        in_specs=[VMEM],
        out_specs=VMEM,
        scratch_shapes=[
            pltpu.VMEM((total, 2 * HD), BF16),
            pltpu.VMEM((HD + 16, total), BF16),
            pltpu.VMEM((2, total, QBLOCK), F32),
            pltpu.VMEM((2, 1, QBLOCK), F32),
        ],
        compiler_params=pltpu.CompilerParams(vmem_limit_bytes=28 << 20),
        cost_estimate=pl.CostEstimate(flops=5 << 30, bytes_accessed=4 << 20, transcendentals=0),
    )(own)


def attend_far(own, other, state, text_kv, length, weight):
    sources, unused, rows, unused2 = own.shape
    words = text_kv.shape[1]
    total = sources * rows + words
    return pl.pallas_call(
        far_kernel,
        out_shape=(
            jax.ShapeDtypeStruct((2, sources, rows // 2, HD), BF16),
            pltpu.VMEM(weight.shape, BF16),
        ),
        in_specs=[VMEM, VMEM, VMEM, ANY, SMEM, ANY],
        out_specs=(VMEM, VMEM),
        scratch_shapes=[
            pltpu.VMEM((total, 2 * HD), BF16),
            pltpu.VMEM((HD + 16, total), BF16),
            pltpu.VMEM((2, total, QBLOCK), F32),
            pltpu.VMEM((2, 1, QBLOCK), F32),
            pltpu.VMEM((2, words, HD), BF16),
            pltpu.SemaphoreType.DMA((3,)),
        ],
        compiler_params=pltpu.CompilerParams(vmem_limit_bytes=40 << 20),
        cost_estimate=pl.CostEstimate(flops=5 << 30, bytes_accessed=12 << 20, transcendentals=0),
    )(own, other, state, text_kv, length, weight)


def final_kernel(
    levels, times, heads, weight, hidden, got, modulation, guide_table, final_t, latent,
    next_out, guided_out, kept_out, sent_out, attention,
    *, count_scale,
):
    width = weight.shape[1]
    cfg_index = lax.axis_index("cfg")
    core = lax.axis_index("seq") % (lax.axis_size("seq") // HEADS)
    branch = cfg_index % 2
    is_cond = branch == 0
    level = levels[cfg_index // 2]
    half = hidden.shape[1] // 2
    for side in range(2):
        for head in range(HEADS):
            attention[pl.ds(side * half, half), pl.ds(head * HD, HD)] = heads[
                side * HEADS + head
            ]
    projected = jnp.dot(attention[...], weight[...], preferred_element_type=F32)
    projected = projected.astype(BF16).astype(F32)
    own_h = hidden[0, pl.ds(pl.multiple_of(branch * half, half), half)].astype(F32)
    got_h = got[:half].astype(F32)
    own_mod = jnp.concatenate([modulation[0], modulation[1], modulation[2]], axis=0)
    parts = got[half:].astype(F32)
    got_mod = parts[:3] + parts[8:11]
    cond_hidden = jnp.where(is_cond, own_h, got_h)
    uncond_hidden = jnp.where(is_cond, got_h, own_h)
    cond_mod = jnp.where(is_cond, own_mod, got_mod)
    uncond_mod = jnp.where(is_cond, got_mod, own_mod)
    cond_proj = projected[:half]

    def layer(hidden, proj, mod):
        normed, inverse = normalize(hidden + mod[0:1] * proj)
        shaped = (normed * (1.0 + mod[2:3]) + mod[1:2]).astype(BF16)
        velocity = lax.dot_general(shaped, final_t[...], NT, preferred_element_type=F32)
        return normed, inverse, shaped, velocity

    cond_vel = layer(cond_hidden, cond_proj, cond_mod)[3]
    uncond_vel = layer(uncond_hidden, projected[half:], uncond_mod)[3]
    factor = 1.0 + GUIDE_STEP * level.astype(F32)
    guided = uncond_vel + factor * (cond_vel - uncond_vel)
    guided_out[0] = guided
    position = jnp.full(guided.shape, times[cfg_index // 2].astype(F32))
    next_out[0] = latent[0] + (sigma_at(position + 1.0) - sigma_at(position)) * guided

    mod = cond_mod + guide_table[level]
    normed, inverse, shaped, velocity = layer(cond_hidden, cond_proj, mod)
    grad_vel = ((velocity - guided) * count_scale).astype(BF16)
    grad_shaped = jnp.dot(grad_vel, final_t[...], preferred_element_type=F32)
    grad_shift = jnp.sum(grad_shaped, axis=0, keepdims=True)
    grad_scale = jnp.sum(grad_shaped * normed, axis=0, keepdims=True)
    grad_norm = grad_shaped * (1.0 + mod[2:3])
    grad_stream = inverse * (
        grad_norm
        - jnp.mean(grad_norm, axis=1, keepdims=True)
        - normed * jnp.mean(grad_norm * normed, axis=1, keepdims=True)
    )
    grad_gate = jnp.sum(grad_stream * cond_proj, axis=0, keepdims=True)
    table = jnp.concatenate(
        [grad_gate, grad_shift, grad_scale, jnp.zeros((13, width), F32)], axis=0
    ).astype(BF16)
    left = jnp.concatenate([shaped, table], axis=0)
    lanes = lax.broadcasted_iota(jnp.int32, (16, 2 * LATC), 1)
    lines = lax.broadcasted_iota(jnp.int32, (16, 2 * LATC), 0)
    unit = (lanes == lines + LATC).astype(F32).astype(BF16)
    right = jnp.concatenate(
        [jnp.concatenate([grad_vel, jnp.zeros_like(grad_vel)], axis=1), unit], axis=0
    )
    terms = lax.dot_general(left, right, TN, preferred_element_type=F32)
    terms = terms.reshape(width // 16, 2, 8, 2 * LATC)
    first = terms[:, 0].reshape(width // 2, 2 * LATC)
    second = terms[:, 1].reshape(width // 2, 2 * LATC)
    on_first = core == 0
    kept_out[...] = jnp.where(on_first, first, second)
    sent_out[...] = jnp.where(on_first, second, first).astype(BF16)


def final_layer(
    levels, times, heads, weight, hidden, got, modulation, guide_table, final_t, latent, count_scale
):
    width = hidden.shape[2]
    half = hidden.shape[1] // 2
    return pl.pallas_call(
        functools.partial(final_kernel, count_scale=count_scale),
        out_shape=(
            jax.ShapeDtypeStruct(latent.shape, F32),
            jax.ShapeDtypeStruct(latent.shape, F32),
            jax.ShapeDtypeStruct((width // 2, 2 * LATC), F32),
            jax.ShapeDtypeStruct((width // 2, 2 * LATC), BF16),
        ),
        in_specs=[SMEM, SMEM] + [VMEM] * 8,
        out_specs=(VMEM, VMEM, VMEM, VMEM),
        scratch_shapes=[pltpu.VMEM((2 * half, HEADS * HD), BF16)],
        compiler_params=pltpu.CompilerParams(vmem_limit_bytes=32 << 20),
        cost_estimate=pl.CostEstimate(flops=1 << 30, bytes_accessed=10 << 20, transcendentals=0),
    )(levels, times, heads, weight, hidden, got, modulation, guide_table, final_t, latent)


def sum_kernel(levels, got, final_out, table_out):
    clips = got.shape[0]
    guides = table_out.shape[2]
    total = None
    planes = [jnp.zeros((8, guides), F32) for unused in range(3)]
    for clip in range(clips):
        block = got[clip].astype(F32).reshape(got.shape[1] // 8, 8, 2 * LATC)
        block = jnp.sum(block, axis=0)
        total = block if total is None else total + block
        picked = lax.broadcasted_iota(jnp.int32, (8, guides), 1) == levels[clip]
        for plane in range(3):
            column = block[:, LATC + plane : LATC + plane + 1]
            planes[plane] = planes[plane] + jnp.where(picked, column, 0.0)
    final_out[...] = total[:, :LATC]
    for plane in range(3):
        table_out[plane] = planes[plane]


def sum_terms(levels, got, guides):
    return pl.pallas_call(
        sum_kernel,
        out_shape=(
            jax.ShapeDtypeStruct((8, LATC), F32),
            jax.ShapeDtypeStruct((3, 8, guides), F32),
        ),
        in_specs=[SMEM, VMEM],
        out_specs=(VMEM, VMEM),
        compiler_params=pltpu.CompilerParams(vmem_limit_bytes=16 << 20),
    )(levels, got)


def local(
    latent,
    query_key_value,
    text_kv,
    text_len,
    hidden,
    modulation,
    out_weight,
    final_weight,
    guide_table,
    time_index,
    guide_index,
):
    seq_count = lax.axis_size("seq")
    cfg_count = lax.axis_size("cfg")
    clips = cfg_count // 2
    tok_rows = query_key_value.shape[1]
    half_rows = tok_rows // 2
    cores = seq_count // HEADS
    mod_rows = modulation.transpose(1, 0, 2)

    sent, passed = pack(query_key_value, hidden, mod_rows)
    same_core = [[cores * i + core for i in range(HEADS)] for core in range(cores)]
    got = lax.all_to_all(
        sent.reshape(HEADS, 3 * tok_rows, HD),
        "seq",
        split_axis=0,
        concat_axis=0,
        tiled=True,
        axis_index_groups=same_core,
    )
    own = got.reshape(HEADS, 3, tok_rows, HD)
    other = lax.ppermute(own, "seq", [(i, i ^ 1) for i in range(seq_count)])
    gotten = lax.ppermute(passed, "cfg", [(i, i ^ 1) for i in range(cfg_count)])
    state = attend_near(own)
    mixed, weight = attend_far(own, other, state, text_kv, text_len, out_weight)
    mixed, gotten = lax.optimization_barrier((mixed, gotten))

    members = 2 * HEADS
    groups = [
        [(g * members + i) * cores + core for i in range(members)]
        for g in range(clips)
        for core in range(cores)
    ]
    heads = lax.all_to_all(
        mixed.reshape(members, half_rows, HD),
        ("cfg", "seq"),
        split_axis=0,
        concat_axis=0,
        tiled=True,
        axis_index_groups=groups,
    )

    count_scale = 1.0 / (clips * tok_rows * seq_count)
    latent_next, guided, kept, given = final_layer(
        guide_index,
        time_index,
        heads,
        weight,
        hidden,
        gotten,
        mod_rows,
        guide_table,
        final_weight.T,
        latent,
        count_scale,
    )
    gained = lax.ppermute(given, "seq", [(i, i ^ 1) for i in range(seq_count)])
    chips = cfg_count * seq_count // cores
    terms = (kept + gained.astype(F32)).astype(BF16)
    pieces = lax.all_to_all(
        terms.reshape(chips, terms.shape[0] // chips, 2 * LATC),
        ("cfg", "seq"),
        split_axis=0,
        concat_axis=0,
        tiled=True,
        axis_index_groups=[[cores * i + core for i in range(chips)] for core in range(cores)],
    )
    final_grad, table = sum_terms(
        guide_index, pieces.reshape(clips, terms.shape[0] // clips, 2 * LATC), guide_table.shape[0]
    )
    return (latent_next, guided, final_grad, table.transpose(2, 0, 1))


def solution(mesh):
    in_specs = (
        P("cfg", "seq", None),
        P("cfg", "seq", None),
        P("cfg", None, None),
        P("cfg"),
        P("cfg", "seq", None),
        P("cfg", None, None),
        P(),
        P(),
        P(),
        P(),
        P(),
    )
    out_specs = (
        P("cfg", "seq", None),
        P("cfg", "seq", None),
        P(("cfg", "seq"), None),
        P(None, None, ("cfg", "seq")),
    )
    return jax.shard_map(local, mesh=mesh, in_specs=in_specs, out_specs=out_specs, check_vma=False)
```

```python
import functools
import math

import jax
import jax.numpy as jnp
from jax import lax
from jax.experimental import pallas as pl
from jax.experimental.pallas import tpu as pltpu
from jax.sharding import PartitionSpec as P

HEADS = 16
HD = 128
STEPS = 50
LATC = 64
NORM_EPS = 1e-06
SHIFT_FACTOR = 7.0
GUIDE_STEP = 0.5

F32 = jnp.float32
BF16 = jnp.bfloat16
VMEM = pl.BlockSpec(memory_space=pltpu.VMEM)
SMEM = pl.BlockSpec(memory_space=pltpu.SMEM)
ANY = pl.BlockSpec(memory_space=pl.ANY)
HBM = pl.BlockSpec(memory_space=pltpu.HBM)
SCORE_SCALE = HD**-0.5 * math.log2(math.e)
NT = (((1,), (1,)), ((), ()))
TN = (((0,), (0,)), ((), ()))


def sigma_at(position):
    frac_left = 1.0 - position / STEPS
    return SHIFT_FACTOR * frac_left / (1.0 + (SHIFT_FACTOR - 1.0) * frac_left)


def normalize(stream):
    average = jnp.mean(stream, axis=-1, keepdims=True)
    centered = stream - average
    inverse = lax.rsqrt(jnp.mean(centered * centered, axis=-1, keepdims=True) + NORM_EPS)
    return centered * inverse, inverse


PIECES = 8


def pack_kernel(packed, hidden, modulation, sent, passed, rows_of_mod, held, sems, late):
    heads, kinds, rows, unused = sent.shape
    half = hidden.shape[1] // 2
    piece = rows // PIECES
    copies = [
        pltpu.make_async_copy(
            packed.at[0, pl.ds(index * piece, piece)],
            held.at[pl.ds(index * piece, piece)],
            sems.at[index],
        )
        for index in range(PIECES)
    ]
    for copy in copies:
        copy.start()
    far = pl.multiple_of((1 - lax.axis_index("cfg") % 2) * half, half)
    rest = pltpu.make_async_copy(
        hidden.at[0, pl.ds(far, half)], passed.at[pl.ds(0, half)], late.at[0]
    )
    rest.start()
    fetch = pltpu.make_async_copy(modulation, rows_of_mod, late.at[1])
    fetch.start()
    fetch.wait()
    mod = jnp.concatenate([rows_of_mod[0], rows_of_mod[1], rows_of_mod[2]], axis=0)
    high = mod.astype(BF16).astype(F32)
    zeros = jnp.zeros((5, mod.shape[1]), F32)
    parts = jnp.concatenate([high, zeros, mod - high, zeros], axis=0)
    passed[pl.ds(half, 16)] = parts.astype(BF16)
    for index in range(PIECES):
        copies[index].wait()
        span = pl.ds(index * piece, piece)
        for kind in range(kinds):
            for head in range(heads):
                column = (kind * heads + head) * HD
                sent[head, kind, span] = held[span, pl.ds(column, HD)]
    rest.wait()


def pack(packed, hidden, modulation):
    rows = packed.shape[1]
    width = hidden.shape[2]
    packed, hidden, modulation = (
        pltpu.with_memory_space_constraint(array, pltpu.HBM)
        for array in (packed, hidden, modulation)
    )
    return pl.pallas_call(
        pack_kernel,
        out_shape=(
            pltpu.VMEM((HEADS, 3, rows, HD), BF16),
            pltpu.VMEM((rows // 2 + 16, width), BF16),
        ),
        in_specs=[HBM, HBM, HBM],
        out_specs=(VMEM, VMEM),
        scratch_shapes=[
            pltpu.VMEM(modulation.shape, F32),
            pltpu.VMEM(packed.shape[1:], BF16),
            pltpu.SemaphoreType.DMA((PIECES,)),
            pltpu.SemaphoreType.DMA((2,)),
        ],
        compiler_params=pltpu.CompilerParams(vmem_limit_bytes=16 << 20),
    )(packed, hidden, modulation)


QBLOCK = 512


def split_query(own, first, count):
    query = own[pl.ds(first, count), 0].reshape(QBLOCK, HD).astype(F32) * SCORE_SCALE
    high = query.astype(BF16)
    low = (query - high.astype(F32)).astype(BF16)
    return jnp.concatenate([high, low], axis=1)


def place_pair(keys, values, first, key, value):
    span = pl.ds(first, key.shape[0])
    keys[span, :HD] = key
    keys[span, HD:] = key
    values[:HD, span] = value.T


def run_steps(steps, score, finish):
    score(0, 0)
    for step in range(steps):
        if step + 1 < steps:
            score(step + 1, (step + 1) % 2)
        finish(step, step % 2)


def near_kernel(own, state, keys, values, scores, tops):
    sources, unused, rows, unused2 = own.shape
    video = sources * rows
    place_pair(keys, values, 0, own[:, 1].reshape(video, HD), own[:, 2].reshape(video, HD))
    values[HD:, :] = jnp.ones((values.shape[0] - HD, video), BF16)
    count = QBLOCK // rows

    def score(step, slot):
        got = lax.dot_general(
            keys[...], split_query(own, step * count, count), NT, preferred_element_type=F32
        )
        scores[slot] = got
        tops[slot] = jnp.max(got, axis=0, keepdims=True)

    def finish(step, slot):
        highest = tops[slot]
        weights = jnp.exp2(scores[slot] - highest).astype(BF16)
        mixed = jnp.dot(values[...], weights, preferred_element_type=F32)
        span = pl.ds(step * QBLOCK, QBLOCK)
        state[: HD + 8, span] = mixed[: HD + 8]
        state[HD + 8 :, span] = jnp.broadcast_to(highest, (8, QBLOCK))

    run_steps(video // QBLOCK, score, finish)


def far_kernel(
    own, other, state, text_kv, length, weight, out, staged, keys, values, scores, tops, text, sems
):
    head = lax.axis_index("seq") // (lax.axis_size("seq") // HEADS)
    text_copies = [
        pltpu.make_async_copy(
            text_kv.at[0, :, pl.ds(pl.multiple_of((kind * HEADS + head) * HD, HD), HD)],
            text.at[kind],
            sems.at[1 + kind],
        )
        for kind in range(2)
    ]
    for copy in text_copies:
        copy.start()
    staging = pltpu.make_async_copy(weight, staged, sems.at[0])
    staging.start()
    sources, unused, rows, unused2 = own.shape
    video = sources * rows
    words = text.shape[1]
    place_pair(keys, values, 0, other[:, 1].reshape(video, HD), other[:, 2].reshape(video, HD))
    for copy in text_copies:
        copy.wait()
    place_pair(keys, values, video, text[0], text[1])
    values[HD:, :] = jnp.ones((values.shape[0] - HD, video + words), BF16)
    kept = lax.broadcasted_iota(jnp.int32, (words, QBLOCK), 0) < length[0]
    count = QBLOCK // rows

    def score(step, slot):
        got = lax.dot_general(
            keys[...], split_query(own, step * count, count), NT, preferred_element_type=F32
        )
        masked = jnp.where(kept, got[video:], -jnp.inf)
        scores[slot, :video] = got[:video]
        scores[slot, video:] = masked
        tops[slot] = jnp.maximum(
            jnp.max(got[:video], axis=0, keepdims=True), jnp.max(masked, axis=0, keepdims=True)
        )

    def finish(step, slot):
        span = pl.ds(step * QBLOCK, QBLOCK)
        before = state[HD + 8 : HD + 9, span]
        highest = jnp.maximum(tops[slot], before)
        weights = jnp.exp2(scores[slot] - highest).astype(BF16)
        mixed = jnp.dot(values[...], weights, preferred_element_type=F32)
        mixed = mixed[: HD + 8] + state[: HD + 8, span] * jnp.exp2(before - highest)
        result = (mixed[:HD] / mixed[HD : HD + 1]).T.astype(BF16)
        result = result.reshape(count, 2, rows // 2, HD)
        span = pl.ds(step * count, count)
        out[0, span] = result[:, 0]
        out[1, span] = result[:, 1]

    run_steps(video // QBLOCK, score, finish)
    staging.wait()


def attend_near(own):
    sources, unused, rows, unused2 = own.shape
    total = sources * rows
    return pl.pallas_call(
        near_kernel,
        out_shape=jax.ShapeDtypeStruct((HD + 16, total), F32),
        in_specs=[VMEM],
        out_specs=VMEM,
        scratch_shapes=[
            pltpu.VMEM((total, 2 * HD), BF16),
            pltpu.VMEM((HD + 16, total), BF16),
            pltpu.VMEM((2, total, QBLOCK), F32),
            pltpu.VMEM((2, 1, QBLOCK), F32),
        ],
        compiler_params=pltpu.CompilerParams(vmem_limit_bytes=28 << 20),
        cost_estimate=pl.CostEstimate(flops=5 << 30, bytes_accessed=4 << 20, transcendentals=0),
    )(own)


def attend_far(own, other, state, text_kv, length, weight):
    sources, unused, rows, unused2 = own.shape
    words = text_kv.shape[1]
    total = sources * rows + words
    return pl.pallas_call(
        far_kernel,
        out_shape=(
            jax.ShapeDtypeStruct((2, sources, rows // 2, HD), BF16),
            pltpu.VMEM(weight.shape, BF16),
        ),
        in_specs=[VMEM, VMEM, VMEM, ANY, SMEM, ANY],
        out_specs=(VMEM, VMEM),
        scratch_shapes=[
            pltpu.VMEM((total, 2 * HD), BF16),
            pltpu.VMEM((HD + 16, total), BF16),
            pltpu.VMEM((2, total, QBLOCK), F32),
            pltpu.VMEM((2, 1, QBLOCK), F32),
            pltpu.VMEM((2, words, HD), BF16),
            pltpu.SemaphoreType.DMA((3,)),
        ],
        compiler_params=pltpu.CompilerParams(vmem_limit_bytes=40 << 20),
        cost_estimate=pl.CostEstimate(flops=5 << 30, bytes_accessed=12 << 20, transcendentals=0),
    )(own, other, state, text_kv, length, weight)


def final_kernel(
    levels, times, heads, weight, hidden, got, modulation, guide_table, final_t, latent,
    next_out, guided_out, kept_out, sent_out, attention,
    *, count_scale,
):
    width = weight.shape[1]
    cfg_index = lax.axis_index("cfg")
    core = lax.axis_index("seq") % (lax.axis_size("seq") // HEADS)
    branch = cfg_index % 2
    is_cond = branch == 0
    level = levels[cfg_index // 2]
    half = hidden.shape[1] // 2
    for side in range(2):
        for head in range(HEADS):
            attention[pl.ds(side * half, half), pl.ds(head * HD, HD)] = heads[
                side * HEADS + head
            ]
    projected = jnp.dot(attention[...], weight[...], preferred_element_type=F32)
    projected = projected.astype(BF16).astype(F32)
    own_h = hidden[0, pl.ds(pl.multiple_of(branch * half, half), half)].astype(F32)
    got_h = got[:half].astype(F32)
    own_mod = jnp.concatenate([modulation[0], modulation[1], modulation[2]], axis=0)
    parts = got[half:].astype(F32)
    got_mod = parts[:3] + parts[8:11]
    cond_hidden = jnp.where(is_cond, own_h, got_h)
    uncond_hidden = jnp.where(is_cond, got_h, own_h)
    cond_mod = jnp.where(is_cond, own_mod, got_mod)
    uncond_mod = jnp.where(is_cond, got_mod, own_mod)
    cond_proj = projected[:half]

    def layer(hidden, proj, mod):
        normed, inverse = normalize(hidden + mod[0:1] * proj)
        shaped = (normed * (1.0 + mod[2:3]) + mod[1:2]).astype(BF16)
        velocity = lax.dot_general(shaped, final_t[...], NT, preferred_element_type=F32)
        return normed, inverse, shaped, velocity

    cond_vel = layer(cond_hidden, cond_proj, cond_mod)[3]
    uncond_vel = layer(uncond_hidden, projected[half:], uncond_mod)[3]
    factor = 1.0 + GUIDE_STEP * level.astype(F32)
    guided = uncond_vel + factor * (cond_vel - uncond_vel)
    guided_out[0] = guided
    position = jnp.full(guided.shape, times[cfg_index // 2].astype(F32))
    next_out[0] = latent[0] + (sigma_at(position + 1.0) - sigma_at(position)) * guided

    mod = cond_mod + guide_table[level]
    normed, inverse, shaped, velocity = layer(cond_hidden, cond_proj, mod)
    grad_vel = ((velocity - guided) * count_scale).astype(BF16)
    grad_shaped = jnp.dot(grad_vel, final_t[...], preferred_element_type=F32)
    grad_shift = jnp.sum(grad_shaped, axis=0, keepdims=True)
    grad_scale = jnp.sum(grad_shaped * normed, axis=0, keepdims=True)
    grad_norm = grad_shaped * (1.0 + mod[2:3])
    grad_stream = inverse * (
        grad_norm
        - jnp.mean(grad_norm, axis=1, keepdims=True)
        - normed * jnp.mean(grad_norm * normed, axis=1, keepdims=True)
    )
    grad_gate = jnp.sum(grad_stream * cond_proj, axis=0, keepdims=True)
    table = jnp.concatenate(
        [grad_gate, grad_shift, grad_scale, jnp.zeros((13, width), F32)], axis=0
    ).astype(BF16)
    left = jnp.concatenate([shaped, table], axis=0)
    lanes = lax.broadcasted_iota(jnp.int32, (16, 2 * LATC), 1)
    lines = lax.broadcasted_iota(jnp.int32, (16, 2 * LATC), 0)
    unit = (lanes == lines + LATC).astype(F32).astype(BF16)
    right = jnp.concatenate(
        [jnp.concatenate([grad_vel, jnp.zeros_like(grad_vel)], axis=1), unit], axis=0
    )
    terms = lax.dot_general(left, right, TN, preferred_element_type=F32)
    terms = terms.reshape(width // 16, 2, 8, 2 * LATC)
    first = terms[:, 0].reshape(width // 2, 2 * LATC)
    second = terms[:, 1].reshape(width // 2, 2 * LATC)
    on_first = core == 0
    kept_out[...] = jnp.where(on_first, first, second)
    sent_out[...] = jnp.where(on_first, second, first).astype(BF16)


def final_layer(
    levels, times, heads, weight, hidden, got, modulation, guide_table, final_t, latent, count_scale
):
    width = hidden.shape[2]
    half = hidden.shape[1] // 2
    return pl.pallas_call(
        functools.partial(final_kernel, count_scale=count_scale),
        out_shape=(
            jax.ShapeDtypeStruct(latent.shape, F32),
            jax.ShapeDtypeStruct(latent.shape, F32),
            jax.ShapeDtypeStruct((width // 2, 2 * LATC), F32),
            jax.ShapeDtypeStruct((width // 2, 2 * LATC), BF16),
        ),
        in_specs=[SMEM, SMEM] + [VMEM] * 8,
        out_specs=(VMEM, VMEM, VMEM, VMEM),
        scratch_shapes=[pltpu.VMEM((2 * half, HEADS * HD), BF16)],
        compiler_params=pltpu.CompilerParams(vmem_limit_bytes=32 << 20),
        cost_estimate=pl.CostEstimate(flops=1 << 30, bytes_accessed=10 << 20, transcendentals=0),
    )(levels, times, heads, weight, hidden, got, modulation, guide_table, final_t, latent)


def sum_kernel(levels, got, final_out, table_out):
    clips = got.shape[0]
    guides = table_out.shape[2]
    total = None
    planes = [jnp.zeros((8, guides), F32) for unused in range(3)]
    for clip in range(clips):
        block = got[clip].astype(F32).reshape(got.shape[1] // 8, 8, 2 * LATC)
        block = jnp.sum(block, axis=0)
        total = block if total is None else total + block
        picked = lax.broadcasted_iota(jnp.int32, (8, guides), 1) == levels[clip]
        for plane in range(3):
            column = block[:, LATC + plane : LATC + plane + 1]
            planes[plane] = planes[plane] + jnp.where(picked, column, 0.0)
    final_out[...] = total[:, :LATC]
    for plane in range(3):
        table_out[plane] = planes[plane]


def sum_terms(levels, got, guides):
    return pl.pallas_call(
        sum_kernel,
        out_shape=(
            jax.ShapeDtypeStruct((8, LATC), F32),
            jax.ShapeDtypeStruct((3, 8, guides), F32),
        ),
        in_specs=[SMEM, VMEM],
        out_specs=(VMEM, VMEM),
        compiler_params=pltpu.CompilerParams(vmem_limit_bytes=16 << 20),
    )(levels, got)


def local(
    latent,
    query_key_value,
    text_kv,
    text_len,
    hidden,
    modulation,
    out_weight,
    final_weight,
    guide_table,
    time_index,
    guide_index,
):
    seq_count = lax.axis_size("seq")
    cfg_count = lax.axis_size("cfg")
    clips = cfg_count // 2
    tok_rows = query_key_value.shape[1]
    half_rows = tok_rows // 2
    cores = seq_count // HEADS
    mod_rows = modulation.transpose(1, 0, 2)

    sent, passed = pack(query_key_value, hidden, mod_rows)
    same_core = [[cores * i + core for i in range(HEADS)] for core in range(cores)]
    got = lax.all_to_all(
        sent.reshape(HEADS, 3 * tok_rows, HD),
        "seq",
        split_axis=0,
        concat_axis=0,
        tiled=True,
        axis_index_groups=same_core,
    )
    own = got.reshape(HEADS, 3, tok_rows, HD)
    other = lax.ppermute(own, "seq", [(i, i ^ 1) for i in range(seq_count)])
    gotten = lax.ppermute(passed, "cfg", [(i, i ^ 1) for i in range(cfg_count)])
    state = attend_near(own)
    mixed, weight = attend_far(own, other, state, text_kv, text_len, out_weight)
    mixed, gotten = lax.optimization_barrier((mixed, gotten))

    members = 2 * HEADS
    groups = [
        [(g * members + i) * cores + core for i in range(members)]
        for g in range(clips)
        for core in range(cores)
    ]
    heads = lax.all_to_all(
        mixed.reshape(members, half_rows, HD),
        ("cfg", "seq"),
        split_axis=0,
        concat_axis=0,
        tiled=True,
        axis_index_groups=groups,
    )

    count_scale = 1.0 / (clips * tok_rows * seq_count)
    latent_next, guided, kept, given = final_layer(
        guide_index,
        time_index,
        heads,
        weight,
        hidden,
        gotten,
        mod_rows,
        guide_table,
        final_weight.T,
        latent,
        count_scale,
    )
    gained = lax.ppermute(given, "seq", [(i, i ^ 1) for i in range(seq_count)])
    chips = cfg_count * seq_count // cores
    terms = (kept + gained.astype(F32)).astype(BF16)
    pieces = lax.all_to_all(
        terms.reshape(chips, terms.shape[0] // chips, 2 * LATC),
        ("cfg", "seq"),
        split_axis=0,
        concat_axis=0,
        tiled=True,
        axis_index_groups=[[cores * i + core for i in range(chips)] for core in range(cores)],
    )
    final_grad, table = sum_terms(
        guide_index, pieces.reshape(clips, terms.shape[0] // clips, 2 * LATC), guide_table.shape[0]
    )
    return (latent_next, guided, final_grad, table.transpose(2, 0, 1))


def solution(mesh):
    in_specs = (
        P("cfg", "seq", None),
        P("cfg", "seq", None),
        P("cfg", None, None),
        P("cfg"),
        P("cfg", "seq", None),
        P("cfg", None, None),
        P(),
        P(),
        P(),
        P(),
        P(),
    )
    out_specs = (
        P("cfg", "seq", None),
        P("cfg", "seq", None),
        P(("cfg", "seq"), None),
        P(None, None, ("cfg", "seq")),
    )
    return jax.shard_map(local, mesh=mesh, in_specs=in_specs, out_specs=out_specs, check_vma=False)
```

```python
import functools
import math

import jax
import jax.numpy as jnp
from jax import lax
from jax.experimental import pallas as pl
from jax.experimental.pallas import tpu as pltpu
from jax.sharding import PartitionSpec as P

HEADS = 16
HD = 128
STEPS = 50
LATC = 64
NORM_EPS = 1e-06
SHIFT_FACTOR = 7.0
GUIDE_STEP = 0.5

F32 = jnp.float32
BF16 = jnp.bfloat16
VMEM = pl.BlockSpec(memory_space=pltpu.VMEM)
SMEM = pl.BlockSpec(memory_space=pltpu.SMEM)
ANY = pl.BlockSpec(memory_space=pl.ANY)
HBM = pl.BlockSpec(memory_space=pltpu.HBM)
SCORE_SCALE = HD**-0.5 * math.log2(math.e)
NT = (((1,), (1,)), ((), ()))
TN = (((0,), (0,)), ((), ()))


def sigma_at(position):
    frac_left = 1.0 - position / STEPS
    return SHIFT_FACTOR * frac_left / (1.0 + (SHIFT_FACTOR - 1.0) * frac_left)


def normalize(stream):
    average = jnp.mean(stream, axis=-1, keepdims=True)
    centered = stream - average
    inverse = lax.rsqrt(jnp.mean(centered * centered, axis=-1, keepdims=True) + NORM_EPS)
    return centered * inverse, inverse


PIECES = 8


def pack_kernel(packed, hidden, modulation, sent, passed, rows_of_mod, held, sems, late):
    heads, kinds, rows, unused = sent.shape
    half = hidden.shape[1] // 2
    piece = rows // PIECES
    copies = [
        pltpu.make_async_copy(
            packed.at[0, pl.ds(index * piece, piece)],
            held.at[pl.ds(index * piece, piece)],
            sems.at[index],
        )
        for index in range(PIECES)
    ]
    far = pl.multiple_of((1 - lax.axis_index("cfg") % 2) * half, half)
    rest = pltpu.make_async_copy(
        hidden.at[0, pl.ds(far, half)], passed.at[pl.ds(0, half)], late.at[0]
    )
    fetch = pltpu.make_async_copy(modulation, rows_of_mod, late.at[1])
    for copy in copies:
        copy.start()
    fetch.start()
    rest.start()
    for index in range(PIECES):
        copies[index].wait()
        span = pl.ds(index * piece, piece)
        for kind in range(kinds):
            for head in range(heads):
                column = (kind * heads + head) * HD
                sent[head, kind, span] = held[span, pl.ds(column, HD)]
    fetch.wait()
    mod = jnp.concatenate([rows_of_mod[0], rows_of_mod[1], rows_of_mod[2]], axis=0)
    high = mod.astype(BF16).astype(F32)
    zeros = jnp.zeros((5, mod.shape[1]), F32)
    parts = jnp.concatenate([high, zeros, mod - high, zeros], axis=0)
    passed[pl.ds(half, 16)] = parts.astype(BF16)
    rest.wait()


def pack(packed, hidden, modulation):
    rows = packed.shape[1]
    width = hidden.shape[2]
    packed, hidden, modulation = (
        pltpu.with_memory_space_constraint(array, pltpu.HBM)
        for array in (packed, hidden, modulation)
    )
    return pl.pallas_call(
        pack_kernel,
        out_shape=(
            pltpu.VMEM((HEADS, 3, rows, HD), BF16),
            pltpu.VMEM((rows // 2 + 16, width), BF16),
        ),
        in_specs=[HBM, HBM, HBM],
        out_specs=(VMEM, VMEM),
        scratch_shapes=[
            pltpu.VMEM(modulation.shape, F32),
            pltpu.VMEM(packed.shape[1:], BF16),
            pltpu.SemaphoreType.DMA((PIECES,)),
            pltpu.SemaphoreType.DMA((2,)),
        ],
        compiler_params=pltpu.CompilerParams(vmem_limit_bytes=16 << 20),
    )(packed, hidden, modulation)


QBLOCK = 512


def split_query(own, first, count):
    query = own[pl.ds(first, count), 0].reshape(QBLOCK, HD).astype(F32) * SCORE_SCALE
    high = query.astype(BF16)
    low = (query - high.astype(F32)).astype(BF16)
    return jnp.concatenate([high, low], axis=1)


def place_pair(keys, values, first, key, value):
    span = pl.ds(first, key.shape[0])
    keys[span, :HD] = key
    keys[span, HD:] = key
    values[:HD, span] = value.T


def run_steps(steps, score, finish):
    score(0, 0)
    for step in range(steps):
        if step + 1 < steps:
            score(step + 1, (step + 1) % 2)
        finish(step, step % 2)


def near_kernel(own, state, keys, values, scores, tops):
    sources, unused, rows, unused2 = own.shape
    video = sources * rows
    place_pair(keys, values, 0, own[:, 1].reshape(video, HD), own[:, 2].reshape(video, HD))
    values[HD:, :] = jnp.ones((values.shape[0] - HD, video), BF16)
    count = QBLOCK // rows

    def score(step, slot):
        got = lax.dot_general(
            keys[...], split_query(own, step * count, count), NT, preferred_element_type=F32
        )
        scores[slot] = got
        tops[slot] = jnp.max(got, axis=0, keepdims=True)

    def finish(step, slot):
        highest = tops[slot]
        weights = jnp.exp2(scores[slot] - highest).astype(BF16)
        mixed = jnp.dot(values[...], weights, preferred_element_type=F32)
        span = pl.ds(step * QBLOCK, QBLOCK)
        state[: HD + 8, span] = mixed[: HD + 8]
        state[HD + 8 :, span] = jnp.broadcast_to(highest, (8, QBLOCK))

    run_steps(video // QBLOCK, score, finish)


def far_kernel(
    own, other, state, text_kv, length, weight, out, staged, keys, values, scores, tops, text, sems
):
    head = lax.axis_index("seq") // (lax.axis_size("seq") // HEADS)
    text_copies = [
        pltpu.make_async_copy(
            text_kv.at[0, :, pl.ds(pl.multiple_of((kind * HEADS + head) * HD, HD), HD)],
            text.at[kind],
            sems.at[1 + kind],
        )
        for kind in range(2)
    ]
    for copy in text_copies:
        copy.start()
    staging = pltpu.make_async_copy(weight, staged, sems.at[0])
    staging.start()
    sources, unused, rows, unused2 = own.shape
    video = sources * rows
    words = text.shape[1]
    place_pair(keys, values, 0, other[:, 1].reshape(video, HD), other[:, 2].reshape(video, HD))
    for copy in text_copies:
        copy.wait()
    place_pair(keys, values, video, text[0], text[1])
    values[HD:, :] = jnp.ones((values.shape[0] - HD, video + words), BF16)
    kept = lax.broadcasted_iota(jnp.int32, (words, QBLOCK), 0) < length[0]
    count = QBLOCK // rows

    def score(step, slot):
        got = lax.dot_general(
            keys[...], split_query(own, step * count, count), NT, preferred_element_type=F32
        )
        masked = jnp.where(kept, got[video:], -jnp.inf)
        scores[slot, :video] = got[:video]
        scores[slot, video:] = masked
        tops[slot] = jnp.maximum(
            jnp.max(got[:video], axis=0, keepdims=True), jnp.max(masked, axis=0, keepdims=True)
        )

    def finish(step, slot):
        span = pl.ds(step * QBLOCK, QBLOCK)
        before = state[HD + 8 : HD + 9, span]
        highest = jnp.maximum(tops[slot], before)
        weights = jnp.exp2(scores[slot] - highest).astype(BF16)
        mixed = jnp.dot(values[...], weights, preferred_element_type=F32)
        mixed = mixed[: HD + 8] + state[: HD + 8, span] * jnp.exp2(before - highest)
        result = (mixed[:HD] / mixed[HD : HD + 1]).T.astype(BF16)
        result = result.reshape(count, 2, rows // 2, HD)
        span = pl.ds(step * count, count)
        out[0, span] = result[:, 0]
        out[1, span] = result[:, 1]

    run_steps(video // QBLOCK, score, finish)
    staging.wait()


def attend_near(own):
    sources, unused, rows, unused2 = own.shape
    total = sources * rows
    return pl.pallas_call(
        near_kernel,
        out_shape=jax.ShapeDtypeStruct((HD + 16, total), F32),
        in_specs=[VMEM],
        out_specs=VMEM,
        scratch_shapes=[
            pltpu.VMEM((total, 2 * HD), BF16),
            pltpu.VMEM((HD + 16, total), BF16),
            pltpu.VMEM((2, total, QBLOCK), F32),
            pltpu.VMEM((2, 1, QBLOCK), F32),
        ],
        compiler_params=pltpu.CompilerParams(vmem_limit_bytes=28 << 20),
        cost_estimate=pl.CostEstimate(flops=5 << 30, bytes_accessed=4 << 20, transcendentals=0),
    )(own)


def attend_far(own, other, state, text_kv, length, weight):
    sources, unused, rows, unused2 = own.shape
    words = text_kv.shape[1]
    total = sources * rows + words
    return pl.pallas_call(
        far_kernel,
        out_shape=(
            jax.ShapeDtypeStruct((2, sources, rows // 2, HD), BF16),
            pltpu.VMEM(weight.shape, BF16),
        ),
        in_specs=[VMEM, VMEM, VMEM, ANY, SMEM, ANY],
        out_specs=(VMEM, VMEM),
        scratch_shapes=[
            pltpu.VMEM((total, 2 * HD), BF16),
            pltpu.VMEM((HD + 16, total), BF16),
            pltpu.VMEM((2, total, QBLOCK), F32),
            pltpu.VMEM((2, 1, QBLOCK), F32),
            pltpu.VMEM((2, words, HD), BF16),
            pltpu.SemaphoreType.DMA((3,)),
        ],
        compiler_params=pltpu.CompilerParams(vmem_limit_bytes=40 << 20),
        cost_estimate=pl.CostEstimate(flops=5 << 30, bytes_accessed=12 << 20, transcendentals=0),
    )(own, other, state, text_kv, length, weight)


def final_kernel(
    levels, times, heads, weight, hidden, got, modulation, guide_table, final_t, latent,
    next_out, guided_out, kept_out, sent_out, attention,
    *, count_scale,
):
    width = weight.shape[1]
    cfg_index = lax.axis_index("cfg")
    core = lax.axis_index("seq") % (lax.axis_size("seq") // HEADS)
    branch = cfg_index % 2
    is_cond = branch == 0
    level = levels[cfg_index // 2]
    half = hidden.shape[1] // 2
    for side in range(2):
        for head in range(HEADS):
            attention[pl.ds(side * half, half), pl.ds(head * HD, HD)] = heads[
                side * HEADS + head
            ]
    projected = jnp.dot(attention[...], weight[...], preferred_element_type=F32)
    projected = projected.astype(BF16).astype(F32)
    own_h = hidden[0, pl.ds(pl.multiple_of(branch * half, half), half)].astype(F32)
    got_h = got[:half].astype(F32)
    own_mod = jnp.concatenate([modulation[0], modulation[1], modulation[2]], axis=0)
    parts = got[half:].astype(F32)
    got_mod = parts[:3] + parts[8:11]
    cond_hidden = jnp.where(is_cond, own_h, got_h)
    uncond_hidden = jnp.where(is_cond, got_h, own_h)
    cond_mod = jnp.where(is_cond, own_mod, got_mod)
    uncond_mod = jnp.where(is_cond, got_mod, own_mod)
    cond_proj = projected[:half]

    def layer(hidden, proj, mod):
        normed, inverse = normalize(hidden + mod[0:1] * proj)
        shaped = (normed * (1.0 + mod[2:3]) + mod[1:2]).astype(BF16)
        velocity = lax.dot_general(shaped, final_t[...], NT, preferred_element_type=F32)
        return normed, inverse, shaped, velocity

    cond_vel = layer(cond_hidden, cond_proj, cond_mod)[3]
    uncond_vel = layer(uncond_hidden, projected[half:], uncond_mod)[3]
    factor = 1.0 + GUIDE_STEP * level.astype(F32)
    guided = uncond_vel + factor * (cond_vel - uncond_vel)
    guided_out[0] = guided
    position = jnp.full(guided.shape, times[cfg_index // 2].astype(F32))
    next_out[0] = latent[0] + (sigma_at(position + 1.0) - sigma_at(position)) * guided

    mod = cond_mod + guide_table[level]
    normed, inverse, shaped, velocity = layer(cond_hidden, cond_proj, mod)
    grad_vel = ((velocity - guided) * count_scale).astype(BF16)
    grad_shaped = jnp.dot(grad_vel, final_t[...], preferred_element_type=F32)
    grad_shift = jnp.sum(grad_shaped, axis=0, keepdims=True)
    grad_scale = jnp.sum(grad_shaped * normed, axis=0, keepdims=True)
    grad_norm = grad_shaped * (1.0 + mod[2:3])
    grad_stream = inverse * (
        grad_norm
        - jnp.mean(grad_norm, axis=1, keepdims=True)
        - normed * jnp.mean(grad_norm * normed, axis=1, keepdims=True)
    )
    grad_gate = jnp.sum(grad_stream * cond_proj, axis=0, keepdims=True)
    table = jnp.concatenate(
        [grad_gate, grad_shift, grad_scale, jnp.zeros((13, width), F32)], axis=0
    ).astype(BF16)
    left = jnp.concatenate([shaped, table], axis=0)
    lanes = lax.broadcasted_iota(jnp.int32, (16, 2 * LATC), 1)
    lines = lax.broadcasted_iota(jnp.int32, (16, 2 * LATC), 0)
    unit = (lanes == lines + LATC).astype(F32).astype(BF16)
    right = jnp.concatenate(
        [jnp.concatenate([grad_vel, jnp.zeros_like(grad_vel)], axis=1), unit], axis=0
    )
    terms = lax.dot_general(left, right, TN, preferred_element_type=F32)
    terms = terms.reshape(width // 16, 2, 8, 2 * LATC)
    first = terms[:, 0].reshape(width // 2, 2 * LATC)
    second = terms[:, 1].reshape(width // 2, 2 * LATC)
    on_first = core == 0
    kept_out[...] = jnp.where(on_first, first, second)
    sent_out[...] = jnp.where(on_first, second, first).astype(BF16)


def final_layer(
    levels, times, heads, weight, hidden, got, modulation, guide_table, final_t, latent, count_scale
):
    width = hidden.shape[2]
    half = hidden.shape[1] // 2
    return pl.pallas_call(
        functools.partial(final_kernel, count_scale=count_scale),
        out_shape=(
            jax.ShapeDtypeStruct(latent.shape, F32),
            jax.ShapeDtypeStruct(latent.shape, F32),
            jax.ShapeDtypeStruct((width // 2, 2 * LATC), F32),
            jax.ShapeDtypeStruct((width // 2, 2 * LATC), BF16),
        ),
        in_specs=[SMEM, SMEM] + [VMEM] * 8,
        out_specs=(VMEM, VMEM, VMEM, VMEM),
        scratch_shapes=[pltpu.VMEM((2 * half, HEADS * HD), BF16)],
        compiler_params=pltpu.CompilerParams(vmem_limit_bytes=32 << 20),
        cost_estimate=pl.CostEstimate(flops=1 << 30, bytes_accessed=10 << 20, transcendentals=0),
    )(levels, times, heads, weight, hidden, got, modulation, guide_table, final_t, latent)


def sum_kernel(levels, got, final_out, table_out):
    clips = got.shape[0]
    guides = table_out.shape[2]
    total = None
    planes = [jnp.zeros((8, guides), F32) for unused in range(3)]
    for clip in range(clips):
        block = got[clip].astype(F32).reshape(got.shape[1] // 8, 8, 2 * LATC)
        block = jnp.sum(block, axis=0)
        total = block if total is None else total + block
        picked = lax.broadcasted_iota(jnp.int32, (8, guides), 1) == levels[clip]
        for plane in range(3):
            column = block[:, LATC + plane : LATC + plane + 1]
            planes[plane] = planes[plane] + jnp.where(picked, column, 0.0)
    final_out[...] = total[:, :LATC]
    for plane in range(3):
        table_out[plane] = planes[plane]


def sum_terms(levels, got, guides):
    return pl.pallas_call(
        sum_kernel,
        out_shape=(
            jax.ShapeDtypeStruct((8, LATC), F32),
            jax.ShapeDtypeStruct((3, 8, guides), F32),
        ),
        in_specs=[SMEM, VMEM],
        out_specs=(VMEM, VMEM),
        compiler_params=pltpu.CompilerParams(vmem_limit_bytes=16 << 20),
    )(levels, got)


def local(
    latent,
    query_key_value,
    text_kv,
    text_len,
    hidden,
    modulation,
    out_weight,
    final_weight,
    guide_table,
    time_index,
    guide_index,
):
    seq_count = lax.axis_size("seq")
    cfg_count = lax.axis_size("cfg")
    clips = cfg_count // 2
    tok_rows = query_key_value.shape[1]
    half_rows = tok_rows // 2
    cores = seq_count // HEADS
    mod_rows = modulation.transpose(1, 0, 2)

    sent, passed = pack(query_key_value, hidden, mod_rows)
    same_core = [[cores * i + core for i in range(HEADS)] for core in range(cores)]
    got = lax.all_to_all(
        sent.reshape(HEADS, 3 * tok_rows, HD),
        "seq",
        split_axis=0,
        concat_axis=0,
        tiled=True,
        axis_index_groups=same_core,
    )
    own = got.reshape(HEADS, 3, tok_rows, HD)
    other = lax.ppermute(own, "seq", [(i, i ^ 1) for i in range(seq_count)])
    gotten = lax.ppermute(passed, "cfg", [(i, i ^ 1) for i in range(cfg_count)])
    state = attend_near(own)
    mixed, weight = attend_far(own, other, state, text_kv, text_len, out_weight)
    mixed, gotten = lax.optimization_barrier((mixed, gotten))

    members = 2 * HEADS
    groups = [
        [(g * members + i) * cores + core for i in range(members)]
        for g in range(clips)
        for core in range(cores)
    ]
    heads = lax.all_to_all(
        mixed.reshape(members, half_rows, HD),
        ("cfg", "seq"),
        split_axis=0,
        concat_axis=0,
        tiled=True,
        axis_index_groups=groups,
    )

    count_scale = 1.0 / (clips * tok_rows * seq_count)
    latent_next, guided, kept, given = final_layer(
        guide_index,
        time_index,
        heads,
        weight,
        hidden,
        gotten,
        mod_rows,
        guide_table,
        final_weight.T,
        latent,
        count_scale,
    )
    gained = lax.ppermute(given, "seq", [(i, i ^ 1) for i in range(seq_count)])
    chips = cfg_count * seq_count // cores
    terms = (kept + gained.astype(F32)).astype(BF16)
    pieces = lax.all_to_all(
        terms.reshape(chips, terms.shape[0] // chips, 2 * LATC),
        ("cfg", "seq"),
        split_axis=0,
        concat_axis=0,
        tiled=True,
        axis_index_groups=[[cores * i + core for i in range(chips)] for core in range(cores)],
    )
    final_grad, table = sum_terms(
        guide_index, pieces.reshape(clips, terms.shape[0] // clips, 2 * LATC), guide_table.shape[0]
    )
    return (latent_next, guided, final_grad, table.transpose(2, 0, 1))


def solution(mesh):
    in_specs = (
        P("cfg", "seq", None),
        P("cfg", "seq", None),
        P("cfg", None, None),
        P("cfg"),
        P("cfg", "seq", None),
        P("cfg", None, None),
        P(),
        P(),
        P(),
        P(),
        P(),
    )
    out_specs = (
        P("cfg", "seq", None),
        P("cfg", "seq", None),
        P(("cfg", "seq"), None),
        P(None, None, ("cfg", "seq")),
    )
    return jax.shard_map(local, mesh=mesh, in_specs=in_specs, out_specs=out_specs, check_vma=False)
```

```python
import functools
import math

import jax
import jax.numpy as jnp
from jax import lax
from jax.experimental import pallas as pl
from jax.experimental.pallas import tpu as pltpu
from jax.sharding import PartitionSpec as P

HEADS = 16
HD = 128
STEPS = 50
LATC = 64
NORM_EPS = 1e-06
SHIFT_FACTOR = 7.0
GUIDE_STEP = 0.5

F32 = jnp.float32
BF16 = jnp.bfloat16
VMEM = pl.BlockSpec(memory_space=pltpu.VMEM)
SMEM = pl.BlockSpec(memory_space=pltpu.SMEM)
ANY = pl.BlockSpec(memory_space=pl.ANY)
HBM = pl.BlockSpec(memory_space=pltpu.HBM)
SCORE_SCALE = HD**-0.5 * math.log2(math.e)
NT = (((1,), (1,)), ((), ()))
TN = (((0,), (0,)), ((), ()))


def sigma_at(position):
    frac_left = 1.0 - position / STEPS
    return SHIFT_FACTOR * frac_left / (1.0 + (SHIFT_FACTOR - 1.0) * frac_left)


def normalize(stream):
    average = jnp.mean(stream, axis=-1, keepdims=True)
    centered = stream - average
    inverse = lax.rsqrt(jnp.mean(centered * centered, axis=-1, keepdims=True) + NORM_EPS)
    return centered * inverse, inverse


PIECES = 8


def pack_kernel(packed, hidden, modulation, sent, passed, rows_of_mod, held, sems, late):
    heads, kinds, rows, unused = sent.shape
    half = hidden.shape[1] // 2
    piece = rows // PIECES
    copies = [
        pltpu.make_async_copy(
            packed.at[0, pl.ds(index * piece, piece)],
            held.at[pl.ds(index * piece, piece)],
            sems.at[index],
        )
        for index in range(PIECES)
    ]
    far = pl.multiple_of((1 - lax.axis_index("cfg") % 2) * half, half)
    rest = pltpu.make_async_copy(
        hidden.at[0, pl.ds(far, half)], passed.at[pl.ds(0, half)], late.at[0]
    )
    fetch = pltpu.make_async_copy(modulation, rows_of_mod, late.at[1])
    fetch.start()
    for copy in copies:
        copy.start()
    rest.start()
    fetch.wait()
    mod = jnp.concatenate([rows_of_mod[0], rows_of_mod[1], rows_of_mod[2]], axis=0)
    high = mod.astype(BF16).astype(F32)
    zeros = jnp.zeros((5, mod.shape[1]), F32)
    parts = jnp.concatenate([high, zeros, mod - high, zeros], axis=0)
    passed[pl.ds(half, 16)] = parts.astype(BF16)
    for index in range(PIECES):
        copies[index].wait()
        span = pl.ds(index * piece, piece)
        for kind in range(kinds):
            for head in range(heads):
                column = (kind * heads + head) * HD
                sent[head, kind, span] = held[span, pl.ds(column, HD)]
    rest.wait()


def pack(packed, hidden, modulation):
    rows = packed.shape[1]
    width = hidden.shape[2]
    packed, hidden, modulation = (
        pltpu.with_memory_space_constraint(array, pltpu.HBM)
        for array in (packed, hidden, modulation)
    )
    return pl.pallas_call(
        pack_kernel,
        out_shape=(
            pltpu.VMEM((HEADS, 3, rows, HD), BF16),
            pltpu.VMEM((rows // 2 + 16, width), BF16),
        ),
        in_specs=[HBM, HBM, HBM],
        out_specs=(VMEM, VMEM),
        scratch_shapes=[
            pltpu.VMEM(modulation.shape, F32),
            pltpu.VMEM(packed.shape[1:], BF16),
            pltpu.SemaphoreType.DMA((PIECES,)),
            pltpu.SemaphoreType.DMA((2,)),
        ],
        compiler_params=pltpu.CompilerParams(vmem_limit_bytes=16 << 20),
    )(packed, hidden, modulation)


QBLOCK = 512


def split_query(own, first, count):
    query = own[pl.ds(first, count), 0].reshape(QBLOCK, HD).astype(F32) * SCORE_SCALE
    high = query.astype(BF16)
    low = (query - high.astype(F32)).astype(BF16)
    return jnp.concatenate([high, low], axis=1)


def place_pair(keys, values, first, key, value):
    span = pl.ds(first, key.shape[0])
    keys[span, :HD] = key
    keys[span, HD:] = key
    values[:HD, span] = value.T


def run_steps(steps, score, finish):
    score(0, 0)
    for step in range(steps):
        if step + 1 < steps:
            score(step + 1, (step + 1) % 2)
        finish(step, step % 2)


def near_kernel(own, state, keys, values, scores, tops):
    sources, unused, rows, unused2 = own.shape
    video = sources * rows
    place_pair(keys, values, 0, own[:, 1].reshape(video, HD), own[:, 2].reshape(video, HD))
    values[HD:, :] = jnp.ones((values.shape[0] - HD, video), BF16)
    count = QBLOCK // rows

    def score(step, slot):
        got = lax.dot_general(
            keys[...], split_query(own, step * count, count), NT, preferred_element_type=F32
        )
        scores[slot] = got
        tops[slot] = jnp.max(got, axis=0, keepdims=True)

    def finish(step, slot):
        highest = tops[slot]
        weights = jnp.exp2(scores[slot] - highest).astype(BF16)
        mixed = jnp.dot(values[...], weights, preferred_element_type=F32)
        span = pl.ds(step * QBLOCK, QBLOCK)
        state[: HD + 8, span] = mixed[: HD + 8]
        state[HD + 8 :, span] = jnp.broadcast_to(highest, (8, QBLOCK))

    run_steps(video // QBLOCK, score, finish)


def far_kernel(
    own, other, state, text_kv, length, weight, out, staged, keys, values, scores, tops, text, sems
):
    head = lax.axis_index("seq") // (lax.axis_size("seq") // HEADS)
    text_copies = [
        pltpu.make_async_copy(
            text_kv.at[0, :, pl.ds(pl.multiple_of((kind * HEADS + head) * HD, HD), HD)],
            text.at[kind],
            sems.at[1 + kind],
        )
        for kind in range(2)
    ]
    for copy in text_copies:
        copy.start()
    staging = pltpu.make_async_copy(weight, staged, sems.at[0])
    staging.start()
    sources, unused, rows, unused2 = own.shape
    video = sources * rows
    words = text.shape[1]
    place_pair(keys, values, 0, other[:, 1].reshape(video, HD), other[:, 2].reshape(video, HD))
    for copy in text_copies:
        copy.wait()
    place_pair(keys, values, video, text[0], text[1])
    values[HD:, :] = jnp.ones((values.shape[0] - HD, video + words), BF16)
    kept = lax.broadcasted_iota(jnp.int32, (words, QBLOCK), 0) < length[0]
    count = QBLOCK // rows

    def score(step, slot):
        got = lax.dot_general(
            keys[...], split_query(own, step * count, count), NT, preferred_element_type=F32
        )
        masked = jnp.where(kept, got[video:], -jnp.inf)
        scores[slot, :video] = got[:video]
        scores[slot, video:] = masked
        tops[slot] = jnp.maximum(
            jnp.max(got[:video], axis=0, keepdims=True), jnp.max(masked, axis=0, keepdims=True)
        )

    def finish(step, slot):
        span = pl.ds(step * QBLOCK, QBLOCK)
        before = state[HD + 8 : HD + 9, span]
        highest = jnp.maximum(tops[slot], before)
        weights = jnp.exp2(scores[slot] - highest).astype(BF16)
        mixed = jnp.dot(values[...], weights, preferred_element_type=F32)
        mixed = mixed[: HD + 8] + state[: HD + 8, span] * jnp.exp2(before - highest)
        result = (mixed[:HD] / mixed[HD : HD + 1]).T.astype(BF16)
        result = result.reshape(count, 2, rows // 2, HD)
        span = pl.ds(step * count, count)
        out[0, span] = result[:, 0]
        out[1, span] = result[:, 1]

    run_steps(video // QBLOCK, score, finish)
    staging.wait()


def attend_near(own):
    sources, unused, rows, unused2 = own.shape
    total = sources * rows
    return pl.pallas_call(
        near_kernel,
        out_shape=jax.ShapeDtypeStruct((HD + 16, total), F32),
        in_specs=[VMEM],
        out_specs=VMEM,
        scratch_shapes=[
            pltpu.VMEM((total, 2 * HD), BF16),
            pltpu.VMEM((HD + 16, total), BF16),
            pltpu.VMEM((2, total, QBLOCK), F32),
            pltpu.VMEM((2, 1, QBLOCK), F32),
        ],
        compiler_params=pltpu.CompilerParams(vmem_limit_bytes=28 << 20),
        cost_estimate=pl.CostEstimate(flops=5 << 30, bytes_accessed=4 << 20, transcendentals=0),
    )(own)


def attend_far(own, other, state, text_kv, length, weight):
    sources, unused, rows, unused2 = own.shape
    words = text_kv.shape[1]
    total = sources * rows + words
    return pl.pallas_call(
        far_kernel,
        out_shape=(
            jax.ShapeDtypeStruct((2, sources, rows // 2, HD), BF16),
            pltpu.VMEM(weight.shape, BF16),
        ),
        in_specs=[VMEM, VMEM, VMEM, ANY, SMEM, ANY],
        out_specs=(VMEM, VMEM),
        scratch_shapes=[
            pltpu.VMEM((total, 2 * HD), BF16),
            pltpu.VMEM((HD + 16, total), BF16),
            pltpu.VMEM((2, total, QBLOCK), F32),
            pltpu.VMEM((2, 1, QBLOCK), F32),
            pltpu.VMEM((2, words, HD), BF16),
            pltpu.SemaphoreType.DMA((3,)),
        ],
        compiler_params=pltpu.CompilerParams(vmem_limit_bytes=40 << 20),
        cost_estimate=pl.CostEstimate(flops=5 << 30, bytes_accessed=12 << 20, transcendentals=0),
    )(own, other, state, text_kv, length, weight)


def final_kernel(
    levels, times, heads, weight, hidden, got, modulation, guide_table, final_t, latent,
    next_out, guided_out, kept_out, sent_out, attention,
    *, count_scale,
):
    width = weight.shape[1]
    cfg_index = lax.axis_index("cfg")
    core = lax.axis_index("seq") % (lax.axis_size("seq") // HEADS)
    branch = cfg_index % 2
    is_cond = branch == 0
    level = levels[cfg_index // 2]
    half = hidden.shape[1] // 2
    for side in range(2):
        for head in range(HEADS):
            attention[pl.ds(side * half, half), pl.ds(head * HD, HD)] = heads[
                side * HEADS + head
            ]
    projected = jnp.dot(attention[...], weight[...], preferred_element_type=F32)
    projected = projected.astype(BF16).astype(F32)
    own_h = hidden[0, pl.ds(pl.multiple_of(branch * half, half), half)].astype(F32)
    got_h = got[:half].astype(F32)
    own_mod = jnp.concatenate([modulation[0], modulation[1], modulation[2]], axis=0)
    parts = got[half:].astype(F32)
    got_mod = parts[:3] + parts[8:11]
    cond_hidden = jnp.where(is_cond, own_h, got_h)
    uncond_hidden = jnp.where(is_cond, got_h, own_h)
    cond_mod = jnp.where(is_cond, own_mod, got_mod)
    uncond_mod = jnp.where(is_cond, got_mod, own_mod)
    cond_proj = projected[:half]

    def layer(hidden, proj, mod):
        normed, inverse = normalize(hidden + mod[0:1] * proj)
        shaped = (normed * (1.0 + mod[2:3]) + mod[1:2]).astype(BF16)
        velocity = lax.dot_general(shaped, final_t[...], NT, preferred_element_type=F32)
        return normed, inverse, shaped, velocity

    cond_vel = layer(cond_hidden, cond_proj, cond_mod)[3]
    uncond_vel = layer(uncond_hidden, projected[half:], uncond_mod)[3]
    factor = 1.0 + GUIDE_STEP * level.astype(F32)
    guided = uncond_vel + factor * (cond_vel - uncond_vel)
    guided_out[0] = guided
    position = jnp.full(guided.shape, times[cfg_index // 2].astype(F32))
    next_out[0] = latent[0] + (sigma_at(position + 1.0) - sigma_at(position)) * guided

    mod = cond_mod + guide_table[level]
    normed, inverse, shaped, velocity = layer(cond_hidden, cond_proj, mod)
    grad_vel = ((velocity - guided) * count_scale).astype(BF16)
    grad_shaped = jnp.dot(grad_vel, final_t[...], preferred_element_type=F32)
    grad_shift = jnp.sum(grad_shaped, axis=0, keepdims=True)
    grad_scale = jnp.sum(grad_shaped * normed, axis=0, keepdims=True)
    grad_norm = grad_shaped * (1.0 + mod[2:3])
    grad_stream = inverse * (
        grad_norm
        - jnp.mean(grad_norm, axis=1, keepdims=True)
        - normed * jnp.mean(grad_norm * normed, axis=1, keepdims=True)
    )
    grad_gate = jnp.sum(grad_stream * cond_proj, axis=0, keepdims=True)
    table = jnp.concatenate(
        [grad_gate, grad_shift, grad_scale, jnp.zeros((13, width), F32)], axis=0
    ).astype(BF16)
    left = jnp.concatenate([shaped, table], axis=0)
    lanes = lax.broadcasted_iota(jnp.int32, (16, 2 * LATC), 1)
    lines = lax.broadcasted_iota(jnp.int32, (16, 2 * LATC), 0)
    unit = (lanes == lines + LATC).astype(F32).astype(BF16)
    right = jnp.concatenate(
        [jnp.concatenate([grad_vel, jnp.zeros_like(grad_vel)], axis=1), unit], axis=0
    )
    terms = lax.dot_general(left, right, TN, preferred_element_type=F32)
    terms = terms.reshape(width // 16, 2, 8, 2 * LATC)
    first = terms[:, 0].reshape(width // 2, 2 * LATC)
    second = terms[:, 1].reshape(width // 2, 2 * LATC)
    on_first = core == 0
    kept_out[...] = jnp.where(on_first, first, second)
    sent_out[...] = jnp.where(on_first, second, first).astype(BF16)


def final_layer(
    levels, times, heads, weight, hidden, got, modulation, guide_table, final_t, latent, count_scale
):
    width = hidden.shape[2]
    half = hidden.shape[1] // 2
    return pl.pallas_call(
        functools.partial(final_kernel, count_scale=count_scale),
        out_shape=(
            jax.ShapeDtypeStruct(latent.shape, F32),
            jax.ShapeDtypeStruct(latent.shape, F32),
            jax.ShapeDtypeStruct((width // 2, 2 * LATC), F32),
            jax.ShapeDtypeStruct((width // 2, 2 * LATC), BF16),
        ),
        in_specs=[SMEM, SMEM] + [VMEM] * 8,
        out_specs=(VMEM, VMEM, VMEM, VMEM),
        scratch_shapes=[pltpu.VMEM((2 * half, HEADS * HD), BF16)],
        compiler_params=pltpu.CompilerParams(vmem_limit_bytes=32 << 20),
        cost_estimate=pl.CostEstimate(flops=1 << 30, bytes_accessed=10 << 20, transcendentals=0),
    )(levels, times, heads, weight, hidden, got, modulation, guide_table, final_t, latent)


def sum_kernel(levels, got, final_out, table_out):
    clips = got.shape[0]
    guides = table_out.shape[2]
    total = None
    planes = [jnp.zeros((8, guides), F32) for unused in range(3)]
    for clip in range(clips):
        block = got[clip].astype(F32).reshape(got.shape[1] // 8, 8, 2 * LATC)
        block = jnp.sum(block, axis=0)
        total = block if total is None else total + block
        picked = lax.broadcasted_iota(jnp.int32, (8, guides), 1) == levels[clip]
        for plane in range(3):
            column = block[:, LATC + plane : LATC + plane + 1]
            planes[plane] = planes[plane] + jnp.where(picked, column, 0.0)
    final_out[...] = total[:, :LATC]
    for plane in range(3):
        table_out[plane] = planes[plane]


def sum_terms(levels, got, guides):
    return pl.pallas_call(
        sum_kernel,
        out_shape=(
            jax.ShapeDtypeStruct((8, LATC), F32),
            jax.ShapeDtypeStruct((3, 8, guides), F32),
        ),
        in_specs=[SMEM, VMEM],
        out_specs=(VMEM, VMEM),
        compiler_params=pltpu.CompilerParams(vmem_limit_bytes=16 << 20),
    )(levels, got)


def local(
    latent,
    query_key_value,
    text_kv,
    text_len,
    hidden,
    modulation,
    out_weight,
    final_weight,
    guide_table,
    time_index,
    guide_index,
):
    seq_count = lax.axis_size("seq")
    cfg_count = lax.axis_size("cfg")
    clips = cfg_count // 2
    tok_rows = query_key_value.shape[1]
    half_rows = tok_rows // 2
    cores = seq_count // HEADS
    mod_rows = modulation.transpose(1, 0, 2)

    sent, passed = pack(query_key_value, hidden, mod_rows)
    same_core = [[cores * i + core for i in range(HEADS)] for core in range(cores)]
    got = lax.all_to_all(
        sent.reshape(HEADS, 3 * tok_rows, HD),
        "seq",
        split_axis=0,
        concat_axis=0,
        tiled=True,
        axis_index_groups=same_core,
    )
    own = got.reshape(HEADS, 3, tok_rows, HD)
    other = lax.ppermute(own, "seq", [(i, i ^ 1) for i in range(seq_count)])
    gotten = lax.ppermute(passed, "cfg", [(i, i ^ 1) for i in range(cfg_count)])
    state = attend_near(own)
    mixed, weight = attend_far(own, other, state, text_kv, text_len, out_weight)
    mixed, gotten = lax.optimization_barrier((mixed, gotten))

    members = 2 * HEADS
    groups = [
        [(g * members + i) * cores + core for i in range(members)]
        for g in range(clips)
        for core in range(cores)
    ]
    heads = lax.all_to_all(
        mixed.reshape(members, half_rows, HD),
        ("cfg", "seq"),
        split_axis=0,
        concat_axis=0,
        tiled=True,
        axis_index_groups=groups,
    )

    count_scale = 1.0 / (clips * tok_rows * seq_count)
    latent_next, guided, kept, given = final_layer(
        guide_index,
        time_index,
        heads,
        weight,
        hidden,
        gotten,
        mod_rows,
        guide_table,
        final_weight.T,
        latent,
        count_scale,
    )
    gained = lax.ppermute(given, "seq", [(i, i ^ 1) for i in range(seq_count)])
    chips = cfg_count * seq_count // cores
    terms = (kept + gained.astype(F32)).astype(BF16)
    pieces = lax.all_to_all(
        terms.reshape(chips, terms.shape[0] // chips, 2 * LATC),
        ("cfg", "seq"),
        split_axis=0,
        concat_axis=0,
        tiled=True,
        axis_index_groups=[[cores * i + core for i in range(chips)] for core in range(cores)],
    )
    final_grad, table = sum_terms(
        guide_index, pieces.reshape(clips, terms.shape[0] // clips, 2 * LATC), guide_table.shape[0]
    )
    return (latent_next, guided, final_grad, table.transpose(2, 0, 1))


def solution(mesh):
    in_specs = (
        P("cfg", "seq", None),
        P("cfg", "seq", None),
        P("cfg", None, None),
        P("cfg"),
        P("cfg", "seq", None),
        P("cfg", None, None),
        P(),
        P(),
        P(),
        P(),
        P(),
    )
    out_specs = (
        P("cfg", "seq", None),
        P("cfg", "seq", None),
        P(("cfg", "seq"), None),
        P(None, None, ("cfg", "seq")),
    )
    return jax.shard_map(local, mesh=mesh, in_specs=in_specs, out_specs=out_specs, check_vma=False)
```
